512 devices in a mesh: depth: 8 (over y), tile: 64 (over z, x, core).
Axes of the slice: x: 4, y: 8, z: 8, core: 2. Of those that a mesh axis runs over, the one named last changes fastest.
Arguments:
- labels: int32 [64, 1024, 1024], P('depth', 'tile'), may hold values from 0 to 255
- depth_order: int32 [64, 8], P('tile'), may hold values from 0 to 7, each once within a row
- opacity_table: int32 [256], replicated, may hold values from 0 to 255
- colour_map: int32 [3, 256], replicated, may hold values from 0 to 255
Outputs:
- frame: float32 [4, 64, 16, 1024], P(None, 'tile', 'depth')
The draws below stay inside these ranges and needn't reach their ends.
Inputs may be any that keep to these rules, and one draw needn't show every extreme that they name: `depth_order`: each row names every rank once.
All inputs are finite; a program needn't handle non-finite values.
Results may differ from the reference program's by a relative error of at most 0.0003.
Values sent between devices are 32-bit elements; how exact they have to be, the bound alone decides.
A program may use at most 64 MiB of HBM per device.

```python
import jax
import jax.numpy as jnp
from jax import lax

LABELS = 256
BX = 1024
BY = 16
BZ = 8
GROUPS = 8
STRIPS = 64
NY = 1024
NZ = 64


def draw_labels(key, part):
    key = jax.random.fold_in(key, 11)
    key_region, key_group, key_loose, key_pick = jax.random.split(key, 4)
    bands = NY // 2
    region_label = jax.random.randint(key_region, (bands, 2), 0, LABELS)
    group_label = jax.random.randint(key_group, (GROUPS, bands, 2), 0, LABELS)
    loose_label = jax.random.randint(key_loose, (NZ, NY, BX), 0, LABELS)
    picker = jax.random.randint(key_pick, (NZ, NY, BX), 0, 4)
    row_band = jnp.arange(NY, dtype=jnp.int32) // 2
    column_half = jnp.arange(BX, dtype=jnp.int32) * 2 // BX
    group_index = jnp.arange(NZ, dtype=jnp.int32) // BZ
    shared = region_label[row_band[:, None], column_half[None, :]]
    own = group_label[group_index[:, None, None], row_band[None, :, None], column_half[None, None, :]]
    result = jnp.where(picker < 2, shared[None], jnp.where(picker == 2, own, loose_label))
    result = result.at[0, 0, 0].set(LABELS - 1)
    result = result.at[0, 0, 1].set(0)
    return result.astype(jnp.int32)


def place_ends(array, own_key, least, top_value):
    longest = array.shape.index(max(array.shape))
    spots = []
    for shift in (0, 1):
        where = [jax.random.randint(jax.random.fold_in(own_key, axis), (), 0, length) for axis, length in enumerate(array.shape)]
        where[longest] = (where[longest] + shift) % array.shape[longest]
        spots.append(tuple(where))
    return array.at[spots[0]].set(least).at[spots[1]].set(top_value)


def setup_inputs(seed: int = 0) -> dict:
    arg_keys = jax.random.split(jax.random.key(seed), 5)
    return {
        "labels": draw_labels(jax.random.fold_in(arg_keys[4], 71), 0),
        "depth_order": jax.vmap(lambda own: jax.random.permutation(own, GROUPS))(jax.random.split(arg_keys[1], STRIPS)).reshape((STRIPS, GROUPS)).astype(jnp.int32),
        "opacity_table": place_ends(jax.random.randint(arg_keys[2], (LABELS,), 0, 256), jax.random.fold_in(arg_keys[2], 1), 0, 255).astype(jnp.int32),
        "colour_map": place_ends(jax.random.randint(arg_keys[3], (3, LABELS), 0, 256), jax.random.fold_in(arg_keys[3], 1), 0, 255).astype(jnp.int32),
    }


LIGHT_Z = 0.8
LIGHT_Y = 0.36
LIGHT_X = 0.48
KEY_VALUE = 0.18

def shading(padded):
    grad_z = 0.5 * (padded[2:, 1:-1, 1:-1] - padded[:-2, 1:-1, 1:-1])
    grad_y = 0.5 * (padded[1:-1, 2:, 1:-1] - padded[1:-1, :-2, 1:-1])
    grad_x = 0.5 * (padded[1:-1, 1:-1, 2:] - padded[1:-1, 1:-1, :-2])
    length = jnp.sqrt(grad_z * grad_z + grad_y * grad_y + grad_x * grad_x)
    facing = jnp.abs(grad_z * LIGHT_Z + grad_y * LIGHT_Y + grad_x * LIGHT_X) / jnp.maximum(length, 0.25)
    return 0.3 + 0.7 * facing

def combine(colours, passes, ranks):
    before = ranks[None, :] < ranks[:, None]
    factors = jnp.where(before[:, :, None, None], passes[None], jnp.float32(1.0))
    ahead = jnp.prod(factors, axis=1)
    return (lax.optimization_barrier(jnp.sum(ahead[None] * colours, axis=1)), jnp.prod(passes, axis=0))

def reference(labels, depth_order, opacity_table, colour_map):
    levels = jnp.concatenate([opacity_table[None, :], colour_map], axis=0).astype(jnp.float32)
    density = jnp.take(levels[0], labels, axis=0) / 255.0
    padded = jnp.pad(density, 1)
    zero_index = jnp.zeros((), jnp.int32)

    def render_strip(inputs):
        strip, ranks = inputs
        first_row = (strip * BY).astype(jnp.int32)
        block = lax.dynamic_slice(padded, (zero_index, first_row, zero_index), (NZ + 2, BY + 2, BX + 2))
        strip_labels = lax.dynamic_slice(labels, (zero_index, first_row, zero_index), (NZ, BY, BX))
        colour = jnp.take(levels[1:], strip_labels, axis=1) / 255.0
        shade = shading(block)
        centre = block[1:-1, 1:-1, 1:-1]
        ramp = 0.5 + ((first_row + jnp.arange(BY, dtype=jnp.int32)).astype(jnp.float32) + 0.5) / NY
        passing = jnp.exp(-2.0 * centre / NZ)
        weight = (1.0 - passing) * shade * ramp[None, :, None]
        samples = (colour * weight[None]).reshape(3, GROUPS, BZ, BY, BX)
        through = jnp.cumprod(passing.reshape(GROUPS, BZ, BY, BX), axis=1)
        ahead_in = jnp.concatenate([jnp.ones_like(through[:, :1]), through[:, :-1]], axis=1)
        brick_colour = lax.optimization_barrier(jnp.sum(ahead_in[None] * samples, axis=2))
        brick_pass = through[:, -1]
        return combine(brick_colour, brick_pass, ranks)
    composite, total_pass = lax.map(render_strip, (jnp.arange(STRIPS, dtype=jnp.int32), depth_order))
    lum = 0.2126 * composite[:, 0] + 0.7152 * composite[:, 1] + 0.0722 * composite[:, 2]
    log_sum = jnp.sum(jnp.log(0.05 + lum))
    scale = KEY_VALUE / jnp.exp(log_sum / (NY * BX))
    mapped = composite * scale / (1.0 + composite * scale)
    return jnp.concatenate([jnp.moveaxis(mapped, 1, 0), (1.0 - total_pass)[None]], axis=0)
```

```python
import functools
import math

import jax
import jax.numpy as jnp
from jax import lax
from jax.experimental import pallas as pl
from jax.experimental.pallas import tpu as pltpu
from jax.sharding import PartitionSpec as P

LIGHT_Z = 0.8
LIGHT_Y = 0.36
LIGHT_X = 0.48
KEY_VALUE = 0.18
INNER = 8
LANES = 128
SUBLANES = 8
MESH = pl.DeviceIdType.MESH


def gathered(table, index):
    return jnp.take_along_axis(table, index, axis=1, mode="promise_in_bounds")


def image_row(labels, z, y):
    blocks, depth_size, rows, lanes = labels.shape
    flat = labels.reshape(blocks * depth_size * rows, lanes)
    return flat[pl.ds(z * rows + y, blocks, stride=depth_size * rows), :]


def kernel(
    sizes,
    labels_hbm,
    order_hbm,
    opacity_hbm,
    colour_hbm,
    frame_ref,
    labels,
    order,
    opacity,
    colour,
    words,
    dens,
    diff_x,
    send_pass,
    send_colour,
    got_pass,
    got_colour,
    part_sums,
    inverse,
    load_sem,
    halo_send,
    halo_recv,
    pass_send,
    pass_recv,
    colour_send,
    colour_recv,
    sum_send,
    sum_recv,
):
    groups, strips, depth_size, rows = sizes
    inner = min(INNER, strips)
    outer = strips // inner
    cols = SUBLANES * LANES
    piece = rows // groups
    me = lax.axis_index("depth")
    tile = lax.axis_index("tile")
    tile_inner = lax.rem(tile, inner)
    tile_outer = tile // inner

    def partner(stage, offset):
        if stage == 0:
            return {"depth": lax.rem(me + offset, groups), "tile": tile}
        if stage == 1:
            return {"depth": me, "tile": tile_outer * inner + lax.rem(tile_inner + offset, inner)}
        return {"depth": me, "tile": lax.rem(tile_outer + offset, outer) * inner + tile_inner}

    stages = ((0, groups), (1, inner), (2, outer))

    loads = [
        pltpu.make_async_copy(
            labels_hbm.at[:, :, pl.ds(block * LANES, LANES)], labels.at[block], load_sem.at[block]
        )
        for block in range(SUBLANES)
    ]
    loads.append(pltpu.make_async_copy(opacity_hbm, opacity, load_sem.at[8]))
    loads.append(pltpu.make_async_copy(colour_hbm, colour, load_sem.at[9]))
    loads.append(pltpu.make_async_copy(order_hbm, order, load_sem.at[10]))
    for load in loads:
        load.start()

    barrier = pltpu.get_barrier_semaphore()
    for stage, count in stages:
        for offset in range(1, count):
            pl.semaphore_signal(
                barrier, inc=1, device_id=partner(stage, offset), device_id_type=MESH
            )
    has_up = tile < strips - 1
    has_down = tile > 0
    has_after = me < groups - 1
    has_before = me > 0

    @pl.when(has_up)
    def _():
        pl.semaphore_signal(
            barrier, inc=1, device_id={"depth": me, "tile": tile + 1}, device_id_type=MESH
        )

    @pl.when(has_down)
    def _():
        pl.semaphore_signal(
            barrier, inc=1, device_id={"depth": me, "tile": tile - 1}, device_id_type=MESH
        )

    for load in loads:
        load.wait()

    level = [opacity[...].reshape(1, 2 * LANES)] + [colour[c : c + 1, :] for c in range(3)]
    packed = level[0] + level[1] * 256 + level[2] * 65536 + level[3] * 16777216
    low = jnp.broadcast_to(packed[:, :LANES], (SUBLANES, LANES))
    high = jnp.broadcast_to(packed[:, LANES:], (SUBLANES, LANES))
    lane = lax.broadcasted_iota(jnp.int32, (SUBLANES, LANES), 1)
    sub = lax.broadcasted_iota(jnp.int32, (SUBLANES, LANES), 0)
    first_lane, last_lane = lane == 0, lane == LANES - 1
    first_cell = first_lane & (sub == 0)
    last_cell = last_lane & (sub == SUBLANES - 1)

    def look_up(z, carry):
        for y in range(rows):
            label = image_row(labels, z, y)
            index = label & (LANES - 1)
            word = jnp.where(label < LANES, gathered(low, index), gathered(high, index))
            words[z, y] = word
            value = (word & 255).astype(jnp.float32)
            dens[z + 1, y + 1] = value
            right = pltpu.roll(value, LANES - 1, 1)
            right = jnp.where(last_lane, pltpu.roll(right, SUBLANES - 1, 0), right)
            right = jnp.where(last_cell, 0.0, right)
            left = pltpu.roll(value, 1, 1)
            left = jnp.where(first_lane, pltpu.roll(left, 1, 0), left)
            left = jnp.where(first_cell, 0.0, left)
            diff_x[z, y] = right - left
        return carry

    lax.fori_loop(0, depth_size, look_up, 0)

    expected = sum(count - 1 for _, count in stages)
    pl.semaphore_wait(
        barrier, expected + has_up.astype(jnp.int32) + has_down.astype(jnp.int32)
    )

    def halo(kind):
        if kind == 0:
            src, dst = (depth_size, pl.ds(1, rows)), (0, pl.ds(1, rows))
            target = {"depth": me + 1, "tile": tile}
        elif kind == 1:
            src, dst = (1, pl.ds(1, rows)), (depth_size + 1, pl.ds(1, rows))
            target = {"depth": me - 1, "tile": tile}
        elif kind == 2:
            src, dst = (pl.ds(1, depth_size), rows), (pl.ds(1, depth_size), 0)
            target = {"depth": me, "tile": tile + 1}
        else:
            src, dst = (pl.ds(1, depth_size), 1), (pl.ds(1, depth_size), rows + 1)
            target = {"depth": me, "tile": tile - 1}
        return pltpu.make_async_remote_copy(
            src_ref=dens.at[src],
            dst_ref=dens.at[dst],
            send_sem=halo_send.at[kind],
            recv_sem=halo_recv.at[kind],
            device_id=target,
            device_id_type=MESH,
        )

    sends = (has_after, has_before, has_up, has_down)
    arrives = (has_before, has_after, has_down, has_up)
    for kind in range(4):

        @pl.when(sends[kind])
        def _(kind=kind):
            halo(kind).start()

    zero = jnp.zeros((SUBLANES, LANES), jnp.float32)

    @pl.when(jnp.logical_not(has_before))
    def _():
        for y in range(rows):
            dens[0, y + 1] = zero

    @pl.when(jnp.logical_not(has_after))
    def _():
        for y in range(rows):
            dens[depth_size + 1, y + 1] = zero

    @pl.when(jnp.logical_not(has_down))
    def _():
        for z in range(depth_size):
            dens[z + 1, 0] = zero

    @pl.when(jnp.logical_not(has_up))
    def _():
        for z in range(depth_size):
            dens[z + 1, rows + 1] = zero

    rate = -2.0 / (255.0 * depth_size * groups)

    def pass_copy(target, source):
        return pltpu.make_async_remote_copy(
            src_ref=send_pass.at[pl.ds(target * piece, piece)],
            dst_ref=got_pass.at[source],
            send_sem=pass_send.at[target],
            recv_sem=pass_recv.at[source],
            device_id={"depth": target, "tile": tile},
            device_id_type=MESH,
        )

    def colour_copy(target, source):
        return pltpu.make_async_remote_copy(
            src_ref=send_colour.at[pl.ds(target * piece, piece)],
            dst_ref=got_colour.at[source],
            send_sem=colour_send.at[target],
            recv_sem=colour_recv.at[source],
            device_id={"depth": target, "tile": tile},
            device_id_type=MESH,
        )

    def turn(step):
        half = (step + 1) // 2
        offset = groups // 2 + jnp.where(lax.rem(step, 2) == 0, half, -half)
        return lax.rem(me + offset + groups, groups)

    def do_pass(step, carry):
        target = turn(step)
        for r in range(piece):
            y = target * piece + r
            total = dens[1, y + 1]
            for z in range(1, depth_size):
                total = total + dens[z + 1, y + 1]
            send_pass[y] = jnp.exp(total * rate)

        @pl.when(target != me)
        def _():
            pass_copy(target, me).start()

        return carry

    lax.fori_loop(0, groups, do_pass, 0)

    for kind in range(4):

        @pl.when(arrives[kind])
        def _(kind=kind):
            halo(kind).wait_recv()

    def do_colour(step, carry):
        target = turn(step)
        for r in range(piece):
            y = target * piece + r
            total = jnp.zeros((SUBLANES, LANES), jnp.float32)
            through = jnp.ones((SUBLANES, LANES), jnp.float32)
            sums = [zero, zero, zero]
            for z in range(depth_size):
                word = words[z, y]
                total = total + dens[z + 1, y + 1]
                after = jnp.exp(total * rate)
                dz = dens[z + 2, y + 1] - dens[z, y + 1]
                dy = dens[z + 1, y + 2] - dens[z + 1, y]
                dx = diff_x[z, y]
                square = dz * dz + dy * dy + dx * dx
                toward = jnp.abs(
                    dz * (0.7 * LIGHT_Z) + dy * (0.7 * LIGHT_Y) + dx * (0.7 * LIGHT_X)
                )
                shade = 0.3 + toward * lax.rsqrt(jnp.maximum(square, (0.25 * 510.0) ** 2))
                weight = (through - after) * shade
                through = after
                for c in range(3):
                    part = lax.shift_right_logical(word, 8 * (c + 1))
                    if c < 2:
                        part = part & 255
                    sums[c] = sums[c] + part.astype(jnp.float32) * weight
            row = (tile * rows + y).astype(jnp.float32)
            ramp = (0.5 + (row + 0.5) / (rows * strips)) / 255.0
            for c in range(3):
                send_colour[y, c] = sums[c] * ramp

        @pl.when(target != me)
        def _():
            colour_copy(target, me).start()

        return carry

    lax.fori_loop(0, groups, do_colour, 0)

    for r in range(piece):
        got_pass[me, r] = send_pass[me * piece + r]
        for c in range(3):
            got_colour[me, r, c] = send_colour[me * piece + r, c]

    for rank in range(groups):
        at = 0
        for g in range(1, groups):
            at = jnp.where(order[0, g] == rank, g, at)
        inverse[rank] = at

    for offset in range(1, groups):
        source = lax.rem(me + offset, groups)
        pass_copy(source, source).wait_recv()
        colour_copy(source, source).wait_recv()

    composite = []
    ahead = []
    for r in range(piece):
        through = jnp.ones((SUBLANES, LANES), jnp.float32)
        sums = [zero, zero, zero]
        for rank in range(groups):
            g = inverse[rank]
            for c in range(3):
                sums[c] = sums[c] + through * got_colour[g, r, c]
            through = through * got_pass[g, r]
        composite.append(sums)
        ahead.append(through)

    logs = zero
    for r in range(piece):
        lum = 0.2126 * composite[r][0] + 0.7152 * composite[r][1] + 0.0722 * composite[r][2]
        logs = logs + jnp.log(0.05 + lum)
    local = jnp.sum(logs, axis=0, keepdims=True)

    for stage, count in stages:
        if count == 1:
            continue
        mine = (me, tile_inner, tile_outer)[stage]
        part_sums[stage, mine] = local

        def sum_copy(target, source, device, stage=stage):
            return pltpu.make_async_remote_copy(
                src_ref=part_sums.at[stage, source],
                dst_ref=part_sums.at[stage, source],
                send_sem=sum_send.at[stage, target],
                recv_sem=sum_recv.at[stage, source],
                device_id=device,
                device_id_type=MESH,
            )

        for offset in range(1, count):
            target = lax.rem(mine + offset, count)
            sum_copy(target, mine, partner(stage, offset)).start()
        for offset in range(1, count):
            source = lax.rem(mine + offset, count)
            sum_copy(source, source, partner(stage, offset)).wait_recv()
        local = part_sums[stage, 0]
        for source in range(1, count):
            local = local + part_sums[stage, source]
    log_sum = jnp.sum(local, axis=1, keepdims=True)
    scale = KEY_VALUE / jnp.exp(log_sum * (1.0 / (rows * strips * cols)))
    scale = jnp.broadcast_to(scale, (SUBLANES, LANES))

    for r in range(piece):
        for c in range(3):
            scaled = composite[r][c] * scale
            frame_ref[c, r] = scaled / (1.0 + scaled)
        frame_ref[3, r] = 1.0 - ahead[r]

    for kind in range(4):

        @pl.when(sends[kind])
        def _(kind=kind):
            halo(kind).wait_send()

    for offset in range(1, groups):
        target = lax.rem(me + offset, groups)
        pass_copy(target, me).wait_send()
        colour_copy(target, me).wait_send()
    for stage, count in stages:
        mine = (me, tile_inner, tile_outer)[stage]
        for offset in range(1, count):
            target = lax.rem(mine + offset, count)
            pltpu.make_async_remote_copy(
                src_ref=part_sums.at[stage, mine],
                dst_ref=part_sums.at[stage, mine],
                send_sem=sum_send.at[stage, target],
                recv_sem=sum_recv.at[stage, mine],
                device_id=partner(stage, offset),
                device_id_type=MESH,
            ).wait_send()


def body(labels, depth_order, opacity_table, colour_map):
    groups = lax.axis_size("depth")
    strips = lax.axis_size("tile")
    depth_size, rows, cols = labels.shape
    piece = rows // groups
    block = (SUBLANES, LANES)
    frame = pl.pallas_call(
        functools.partial(kernel, (groups, strips, depth_size, rows)),
        out_shape=jax.ShapeDtypeStruct((4, piece) + block, jnp.float32),
        in_specs=[pl.BlockSpec(memory_space=pl.ANY)] * 4,
        out_specs=pl.BlockSpec(memory_space=pltpu.VMEM),
        scratch_shapes=[
            pltpu.VMEM((SUBLANES, depth_size, rows, LANES), jnp.int32),
            pltpu.SMEM((1, groups), jnp.int32),
            pltpu.VMEM((2 * LANES,), jnp.int32),
            pltpu.VMEM((3, 2 * LANES), jnp.int32),
            pltpu.VMEM((depth_size, rows) + block, jnp.int32),
            pltpu.VMEM((depth_size + 2, rows + 2) + block, jnp.float32),
            pltpu.VMEM((depth_size, rows) + block, jnp.float32),
            pltpu.VMEM((rows,) + block, jnp.float32),
            pltpu.VMEM((rows, 3) + block, jnp.float32),
            pltpu.VMEM((groups, piece) + block, jnp.float32),
            pltpu.VMEM((groups, piece, 3) + block, jnp.float32),
            pltpu.VMEM((3, 8, 1, LANES), jnp.float32),
            pltpu.SMEM((groups,), jnp.int32),
            pltpu.SemaphoreType.DMA((11,)),
            pltpu.SemaphoreType.DMA((4,)),
            pltpu.SemaphoreType.DMA((4,)),
            pltpu.SemaphoreType.DMA((groups,)),
            pltpu.SemaphoreType.DMA((groups,)),
            pltpu.SemaphoreType.DMA((groups,)),
            pltpu.SemaphoreType.DMA((groups,)),
            pltpu.SemaphoreType.DMA((3, 8)),
            pltpu.SemaphoreType.DMA((3, 8)),
        ],
        compiler_params=pltpu.CompilerParams(
            collective_id=0, has_side_effects=True, vmem_limit_bytes=60 * 1024 * 1024
        ),
        name="render",
    )(labels, depth_order, opacity_table, colour_map)
    return frame.reshape(4, 1, piece, cols)


def solution(mesh):
    in_specs = (P("depth", "tile", None), P("tile", None), P(), P())
    out_specs = P(None, "tile", "depth", None)
    return jax.shard_map(body, mesh=mesh, in_specs=in_specs, out_specs=out_specs, check_vma=False)
```

```python
import functools

import jax
import jax.numpy as jnp
from jax import lax
from jax.experimental import pallas as pl
from jax.experimental.pallas import tpu as pltpu
from jax.sharding import PartitionSpec as P

LIGHT_Z = 0.8
LIGHT_Y = 0.36
LIGHT_X = 0.48
KEY_VALUE = 0.18
SIZE_X = 4
LANES = 128
SUBLANES = 8
MESH = pl.DeviceIdType.MESH


def gathered(table, index):
    return jnp.take_along_axis(table, index, axis=1, mode="promise_in_bounds")


def image_row(labels, z, y):
    blocks, depth_size, rows, lanes = labels.shape
    flat = labels.reshape(blocks * depth_size * rows, lanes)
    return flat[pl.ds(z * rows + y, blocks, stride=depth_size * rows), :]


def kernel(
    sizes,
    labels_hbm,
    order_hbm,
    opacity_hbm,
    colour_hbm,
    frame_ref,
    labels,
    order,
    opacity,
    colour,
    words,
    dens,
    send_pass,
    send_colour,
    got_pass,
    got_colour,
    part_one,
    part_two,
    inverse,
    load_sem,
    halo_send,
    halo_recv,
    block_send,
    block_recv,
    sum_send,
    sum_recv,
    rounds,
):
    groups, strips, depth_size, rows = sizes
    cols = SUBLANES * LANES
    piece = rows // groups
    size_x = min(SIZE_X, strips // 2)
    size_z = strips // (2 * size_x)
    me = lax.axis_index("depth")
    tile = lax.axis_index("tile")
    chip = tile // 2
    core = lax.rem(tile, 2)
    at_x = lax.rem(chip, size_x)
    at_z = chip // size_x
    lengths = {"y": groups, "x": size_x, "z": size_z}

    def along(axis, offset):
        if axis == "y":
            return {"depth": lax.rem(me + offset, groups), "tile": tile}
        if axis == "x":
            there = at_z * size_x + lax.rem(at_x + offset, size_x)
        else:
            there = lax.rem(at_z + offset, size_z) * size_x + at_x
        return {"depth": me, "tile": there * 2 + core}

    def greet(semaphore, device):
        pl.semaphore_signal(semaphore, inc=1, device_id=device, device_id_type=MESH)

    barrier = pltpu.get_barrier_semaphore()
    has_up = tile < strips - 1
    has_down = tile > 0
    has_after = me < groups - 1
    has_before = me > 0
    other_core = {"depth": me, "tile": tile + 1 - 2 * core}
    near = [(a, o) for a, n in lengths.items() if n > 1 for o in sorted({1, n - 1})]
    for axis, offset in near:
        greet(barrier, along(axis, offset))
    greet(barrier, other_core)
    beside = jnp.where(core == 0, tile - 1, tile + 1)
    has_beside = (beside >= 0) & (beside < strips)

    @pl.when(has_beside)
    def _():
        greet(barrier, {"depth": me, "tile": beside})

    for block in range(SUBLANES):
        pltpu.make_async_copy(
            labels_hbm.at[:, :, pl.ds(block * LANES, LANES)], labels.at[block], load_sem.at[0]
        ).start()
    loads = [
        pltpu.make_async_copy(opacity_hbm, opacity, load_sem.at[1]),
        pltpu.make_async_copy(colour_hbm, colour, load_sem.at[2]),
        pltpu.make_async_copy(order_hbm, order, load_sem.at[3]),
    ]
    for load in loads:
        load.start()
    for load in loads:
        load.wait()

    level = [opacity[...].reshape(1, 2 * LANES)] + [colour[c : c + 1, :] for c in range(3)]
    packed = level[0] + level[1] * 256 + level[2] * 65536 + level[3] * 16777216
    low = jnp.broadcast_to(packed[:, :LANES], (SUBLANES, LANES))
    high = jnp.broadcast_to(packed[:, LANES:], (SUBLANES, LANES))
    lane = lax.broadcasted_iota(jnp.int32, (SUBLANES, LANES), 1)
    sub = lax.broadcasted_iota(jnp.int32, (SUBLANES, LANES), 0)
    first_lane, last_lane = lane == 0, lane == LANES - 1
    first_cell = first_lane & (sub == 0)
    last_cell = last_lane & (sub == SUBLANES - 1)
    zero = jnp.zeros((SUBLANES, LANES), jnp.float32)
    one = jnp.ones((SUBLANES, LANES), jnp.float32)
    pltpu.make_async_copy(labels, labels, load_sem.at[0]).wait()

    def look_up(z, y):
        label = image_row(labels, z, y)
        index = label & (LANES - 1)
        word = jnp.where(label < LANES, gathered(low, index), gathered(high, index))
        words[z, y] = word
        dens[z + 1, y + 1] = (word & 255).astype(jnp.float32)

    def halo(kind):
        if kind == 0:
            src, dst = (depth_size, pl.ds(1, rows)), (0, pl.ds(1, rows))
            target = {"depth": me + 1, "tile": tile}
        elif kind == 1:
            src, dst = (1, pl.ds(1, rows)), (depth_size + 1, pl.ds(1, rows))
            target = {"depth": me - 1, "tile": tile}
        elif kind == 2:
            src, dst = (pl.ds(1, depth_size), rows), (pl.ds(1, depth_size), 0)
            target = {"depth": me, "tile": tile + 1}
        else:
            src, dst = (pl.ds(1, depth_size), 1), (pl.ds(1, depth_size), rows + 1)
            target = {"depth": me, "tile": tile - 1}
        return pltpu.make_async_remote_copy(
            src_ref=dens.at[src],
            dst_ref=dens.at[dst],
            send_sem=halo_send.at[kind],
            recv_sem=halo_recv.at[kind],
            device_id=target,
            device_id_type=MESH,
        )

    sends = (has_after, has_before, has_up, has_down)
    arrives = (has_before, has_after, has_down, has_up)

    def start_halo(kind):
        @pl.when(sends[kind])
        def _():
            halo(kind).start()

    for y in range(rows):
        look_up(depth_size - 1, y)
        look_up(0, y)
    pl.semaphore_wait(barrier, len(near) + 1 + has_beside.astype(jnp.int32))
    start_halo(0)
    start_halo(1)
    first_round = [(a, o) for a, o in near if lengths[a] >= 4]
    for axis, offset in first_round:
        greet(rounds.at[0], along(axis, offset))
    for z in range(1, depth_size - 1):
        look_up(z, 0)
        look_up(z, rows - 1)
    start_halo(2)
    start_halo(3)

    @pl.when(jnp.logical_not(has_before))
    def _():
        for y in range(rows):
            dens[0, y + 1] = zero

    @pl.when(jnp.logical_not(has_after))
    def _():
        for y in range(rows):
            dens[depth_size + 1, y + 1] = zero

    @pl.when(jnp.logical_not(has_down))
    def _():
        for z in range(depth_size):
            dens[z + 1, 0] = zero

    @pl.when(jnp.logical_not(has_up))
    def _():
        for z in range(depth_size):
            dens[z + 1, rows + 1] = zero

    def look_up_layer(z, carry):
        for y in range(1, rows - 1):
            look_up(z, y)
        return carry

    lax.fori_loop(1, depth_size - 1, look_up_layer, 0)

    rate = -2.0 / (255.0 * depth_size * groups)
    for y in range(rows):
        total = dens[1, y + 1]
        for z in range(1, depth_size):
            total = total + dens[z + 1, y + 1]
        send_pass[y] = jnp.exp(total * rate)

    if first_round:
        pl.semaphore_wait(rounds.at[0], len(first_round))
    second_round = [(a, o) for a, n in lengths.items() if n >= 8 for o in (2, n - 2)]
    for axis, offset in second_round:
        greet(rounds.at[1], along(axis, offset))
    if second_round:
        pl.semaphore_wait(rounds.at[1], len(second_round))
    third_round = [("x", o) for o in range(1, size_x)] if size_z > 1 else []
    for axis, offset in third_round:
        greet(rounds.at[2], along(axis, offset))

    def block_copy(sent, got, which, target):
        return pltpu.make_async_remote_copy(
            src_ref=sent.at[pl.ds(target * piece, piece)],
            dst_ref=got.at[me],
            send_sem=block_send.at[which],
            recv_sem=block_recv.at[which],
            device_id={"depth": target, "tile": tile},
            device_id_type=MESH,
        )

    def turn(step):
        half = (step + 1) // 2
        offset = groups // 2 + jnp.where(lax.rem(step, 2) == 0, half, -half)
        return lax.rem(me + offset + groups, groups)

    def pass_block(step, carry):
        block_copy(send_pass, got_pass, 0, turn(step)).start()
        return carry

    lax.fori_loop(0, groups - 1, pass_block, 0)

    for kind in range(4):

        @pl.when(arrives[kind])
        def _(kind=kind):
            halo(kind).wait_recv()

    def do_colour(step, carry):
        target = turn(step)
        for r in range(piece):
            y = target * piece + r
            total = zero
            through = one
            sums = [zero, zero, zero]
            for z in range(depth_size):
                word = words[z, y]
                value = dens[z + 1, y + 1]
                total = total + value
                after = jnp.exp(total * rate)
                right = pltpu.roll(value, LANES - 1, 1)
                right = jnp.where(last_lane, pltpu.roll(right, SUBLANES - 1, 0), right)
                right = jnp.where(last_cell, 0.0, right)
                left = pltpu.roll(value, 1, 1)
                left = jnp.where(first_lane, pltpu.roll(left, 1, 0), left)
                left = jnp.where(first_cell, 0.0, left)
                dz = dens[z + 2, y + 1] - dens[z, y + 1]
                dy = dens[z + 1, y + 2] - dens[z + 1, y]
                dx = right - left
                square = dz * dz + dy * dy + dx * dx
                toward = jnp.abs(
                    dz * (0.7 * LIGHT_Z) + dy * (0.7 * LIGHT_Y) + dx * (0.7 * LIGHT_X)
                )
                shade = 0.3 + toward * lax.rsqrt(jnp.maximum(square, (0.25 * 510.0) ** 2))
                weight = (through - after) * shade
                through = after
                for c in range(3):
                    part = lax.shift_right_logical(word, 8 * (c + 1))
                    if c < 2:
                        part = part & 255
                    sums[c] = sums[c] + part.astype(jnp.float32) * weight
            row = (tile * rows + y).astype(jnp.float32)
            ramp = (0.5 + (row + 0.5) / (rows * strips)) / 255.0
            for c in range(3):
                send_colour[y, c] = sums[c] * ramp

        @pl.when(target != me)
        def _():
            block_copy(send_colour, got_colour, 1, target).start()

        return carry

    lax.fori_loop(0, groups, do_colour, 0)

    for r in range(piece):
        got_pass[me, r] = send_pass[me * piece + r]
        for c in range(3):
            got_colour[me, r, c] = send_colour[me * piece + r, c]

    for rank in range(groups):
        at = 0
        for g in range(1, groups):
            at = jnp.where(order[0, g] == rank, g, at)
        inverse[rank] = at

    if third_round:
        pl.semaphore_wait(rounds.at[2], len(third_round))

    def all_but_one(ref, semaphore):
        part = ref.at[pl.ds(0, ref.shape[0] - 1)]
        return pltpu.make_async_copy(part, part, semaphore)

    all_but_one(got_pass, block_recv.at[0]).wait()
    all_but_one(got_colour, block_recv.at[1]).wait()

    composite = []
    ahead = []
    for r in range(piece):
        through = one
        sums = [zero, zero, zero]
        for rank in range(groups):
            g = inverse[rank]
            for c in range(3):
                sums[c] = sums[c] + through * got_colour[g, r, c]
            through = through * got_pass[g, r]
        composite.append(sums)
        ahead.append(through)

    logs = zero
    for r in range(piece):
        lum = 0.2126 * composite[r][0] + 0.7152 * composite[r][1] + 0.0722 * composite[r][2]
        logs = logs + jnp.log(0.05 + lum)
    local = jnp.sum(logs, axis=0, keepdims=True)

    def in_first(index):
        return {"depth": index // 2, "tile": chip * 2 + lax.rem(index, 2)}

    def in_second(index):
        return {"depth": me, "tile": index * 2 + core}

    stages = ((part_one, me * 2 + core, in_first), (part_two, chip, in_second))
    for stage, (parts, mine, device) in enumerate(stages):
        count = parts.shape[0]
        parts[mine] = local
        for offset in range(1, count):
            pltpu.make_async_remote_copy(
                src_ref=parts.at[mine],
                dst_ref=parts.at[mine],
                send_sem=sum_send.at[stage],
                recv_sem=sum_recv.at[stage],
                device_id=device(lax.rem(mine + offset, count)),
                device_id_type=MESH,
            ).start()
        all_but_one(parts, sum_recv.at[stage]).wait()
        local = jnp.sum(parts[...], axis=0)
    log_sum = jnp.sum(local, axis=1, keepdims=True)
    scale = KEY_VALUE / jnp.exp(log_sum * (1.0 / (rows * strips * cols)))
    scale = jnp.broadcast_to(scale, (SUBLANES, LANES))

    for r in range(piece):
        for c in range(3):
            scaled = composite[r][c] * scale
            frame_ref[c, r] = scaled / (1.0 + scaled)
        frame_ref[3, r] = 1.0 - ahead[r]

    for kind in range(4):

        @pl.when(sends[kind])
        def _(kind=kind):
            halo(kind).wait_send()

    all_but_one(got_pass, block_send.at[0]).wait()
    all_but_one(got_colour, block_send.at[1]).wait()
    all_but_one(part_one, sum_send.at[0]).wait()
    all_but_one(part_two, sum_send.at[1]).wait()


def body(labels, depth_order, opacity_table, colour_map):
    groups = lax.axis_size("depth")
    strips = lax.axis_size("tile")
    depth_size, rows, cols = labels.shape
    piece = rows // groups
    block = (SUBLANES, LANES)
    frame = pl.pallas_call(
        functools.partial(kernel, (groups, strips, depth_size, rows)),
        out_shape=jax.ShapeDtypeStruct((4, piece) + block, jnp.float32),
        in_specs=[pl.BlockSpec(memory_space=pl.ANY)] * 4,
        out_specs=pl.BlockSpec(memory_space=pltpu.VMEM),
        scratch_shapes=[
            pltpu.VMEM((SUBLANES, depth_size, rows, LANES), jnp.int32),
            pltpu.SMEM((1, groups), jnp.int32),
            pltpu.VMEM((2 * LANES,), jnp.int32),
            pltpu.VMEM((3, 2 * LANES), jnp.int32),
            pltpu.VMEM((depth_size, rows) + block, jnp.int32),
            pltpu.VMEM((depth_size + 2, rows + 2) + block, jnp.float32),
            pltpu.VMEM((rows,) + block, jnp.float32),
            pltpu.VMEM((rows, 3) + block, jnp.float32),
            pltpu.VMEM((groups, piece) + block, jnp.float32),
            pltpu.VMEM((groups, piece, 3) + block, jnp.float32),
            pltpu.VMEM((groups * 2, 1, LANES), jnp.float32),
            pltpu.VMEM((strips // 2, 1, LANES), jnp.float32),
            pltpu.SMEM((groups,), jnp.int32),
            pltpu.SemaphoreType.DMA((4,)),
            pltpu.SemaphoreType.DMA((4,)),
            pltpu.SemaphoreType.DMA((4,)),
            pltpu.SemaphoreType.DMA((2,)),
            pltpu.SemaphoreType.DMA((2,)),
            pltpu.SemaphoreType.DMA((2,)),
            pltpu.SemaphoreType.DMA((2,)),
            pltpu.SemaphoreType.REGULAR((3,)),
        ],
        compiler_params=pltpu.CompilerParams(
            collective_id=0, has_side_effects=True, vmem_limit_bytes=60 * 1024 * 1024
        ),
        name="render",
    )(labels, depth_order, opacity_table, colour_map)
    return frame.reshape(4, 1, piece, cols)


def solution(mesh):
    in_specs = (P("depth", "tile", None), P("tile", None), P(), P())
    out_specs = P(None, "tile", "depth", None)
    return jax.shard_map(body, mesh=mesh, in_specs=in_specs, out_specs=out_specs, check_vma=False)
```

```python
import functools

import jax
import jax.numpy as jnp
from jax import lax
from jax.experimental import pallas as pl
from jax.experimental.pallas import tpu as pltpu
from jax.sharding import PartitionSpec as P

LIGHT_Z = 0.8
LIGHT_Y = 0.36
LIGHT_X = 0.48
KEY_VALUE = 0.18
SIZE_X = 4
LANES = 128
SUBLANES = 8
MESH = pl.DeviceIdType.MESH


def gathered(table, index):
    return jnp.take_along_axis(table, index, axis=1, mode="promise_in_bounds")


def image_row(labels, z, y):
    blocks, depth_size, rows, lanes = labels.shape
    flat = labels.reshape(blocks * depth_size * rows, lanes)
    return flat[pl.ds(z * rows + y, blocks, stride=depth_size * rows), :]


def kernel(
    sizes,
    labels_hbm,
    order_hbm,
    opacity_hbm,
    colour_hbm,
    frame_ref,
    labels,
    order,
    opacity,
    colour,
    words,
    dens,
    send_pass,
    send_colour,
    got_pass,
    got_colour,
    part_one,
    part_two,
    inverse,
    load_sem,
    halo_send,
    halo_recv,
    block_send,
    block_recv,
    sum_send,
    sum_recv,
    rounds,
):
    groups, strips, depth_size, rows = sizes
    cols = SUBLANES * LANES
    piece = rows // groups
    size_x = min(SIZE_X, strips // 2)
    size_z = strips // (2 * size_x)
    me = lax.axis_index("depth")
    tile = lax.axis_index("tile")
    chip = tile // 2
    core = lax.rem(tile, 2)
    at_x = lax.rem(chip, size_x)
    at_z = chip // size_x
    lengths = {"y": groups, "x": size_x, "z": size_z}

    def along(axis, offset):
        if axis == "y":
            return {"depth": lax.rem(me + offset, groups), "tile": tile}
        if axis == "x":
            there = at_z * size_x + lax.rem(at_x + offset, size_x)
        else:
            there = lax.rem(at_z + offset, size_z) * size_x + at_x
        return {"depth": me, "tile": there * 2 + core}

    def greet(semaphore, device):
        pl.semaphore_signal(semaphore, inc=1, device_id=device, device_id_type=MESH)

    barrier = pltpu.get_barrier_semaphore()
    has_up = tile < strips - 1
    has_down = tile > 0
    has_after = me < groups - 1
    has_before = me > 0
    other_core = {"depth": me, "tile": tile + 1 - 2 * core}
    near = [(a, o) for a, n in lengths.items() if n > 1 for o in sorted({1, n - 1})]
    for axis, offset in near:
        greet(barrier, along(axis, offset))
    greet(barrier, other_core)
    beside = jnp.where(core == 0, tile - 1, tile + 1)
    has_beside = (beside >= 0) & (beside < strips)

    @pl.when(has_beside)
    def _():
        greet(barrier, {"depth": me, "tile": beside})

    for block in range(SUBLANES):
        pltpu.make_async_copy(
            labels_hbm.at[:, :, pl.ds(block * LANES, LANES)], labels.at[block], load_sem.at[0]
        ).start()
    loads = [
        pltpu.make_async_copy(opacity_hbm, opacity, load_sem.at[1]),
        pltpu.make_async_copy(colour_hbm, colour, load_sem.at[2]),
        pltpu.make_async_copy(order_hbm, order, load_sem.at[3]),
    ]
    for load in loads:
        load.start()
    for load in loads:
        load.wait()

    level = [opacity[...].reshape(1, 2 * LANES)] + [colour[c : c + 1, :] for c in range(3)]
    packed = level[0] + level[1] * 256 + level[2] * 65536 + level[3] * 16777216
    low = jnp.broadcast_to(packed[:, :LANES], (SUBLANES, LANES))
    high = jnp.broadcast_to(packed[:, LANES:], (SUBLANES, LANES))
    lane = lax.broadcasted_iota(jnp.int32, (SUBLANES, LANES), 1)
    sub = lax.broadcasted_iota(jnp.int32, (SUBLANES, LANES), 0)
    first_lane, last_lane = lane == 0, lane == LANES - 1
    first_cell = first_lane & (sub == 0)
    last_cell = last_lane & (sub == SUBLANES - 1)
    zero = jnp.zeros((SUBLANES, LANES), jnp.float32)
    one = jnp.ones((SUBLANES, LANES), jnp.float32)
    pltpu.make_async_copy(labels, labels, load_sem.at[0]).wait()

    def look_up(z, y):
        label = image_row(labels, z, y)
        index = label & (LANES - 1)
        word = jnp.where(label < LANES, gathered(low, index), gathered(high, index))
        words[z, y] = word
        dens[z + 1, y + 1] = (word & 255).astype(jnp.float32)

    def halo(kind):
        if kind == 0:
            src, dst = (depth_size, pl.ds(1, rows)), (0, pl.ds(1, rows))
            target = {"depth": me + 1, "tile": tile}
        elif kind == 1:
            src, dst = (1, pl.ds(1, rows)), (depth_size + 1, pl.ds(1, rows))
            target = {"depth": me - 1, "tile": tile}
        elif kind == 2:
            src, dst = (pl.ds(1, depth_size), rows), (pl.ds(1, depth_size), 0)
            target = {"depth": me, "tile": tile + 1}
        else:
            src, dst = (pl.ds(1, depth_size), 1), (pl.ds(1, depth_size), rows + 1)
            target = {"depth": me, "tile": tile - 1}
        return pltpu.make_async_remote_copy(
            src_ref=dens.at[src],
            dst_ref=dens.at[dst],
            send_sem=halo_send.at[kind],
            recv_sem=halo_recv.at[kind],
            device_id=target,
            device_id_type=MESH,
        )

    sends = (has_after, has_before, has_up, has_down)
    arrives = (has_before, has_after, has_down, has_up)

    def start_halo(kind):
        @pl.when(sends[kind])
        def _():
            halo(kind).start()

    for y in range(rows):
        look_up(depth_size - 1, y)
        look_up(0, y)
    pl.semaphore_wait(barrier, len(near) + 1 + has_beside.astype(jnp.int32))
    start_halo(0)
    start_halo(1)
    first_round = [(a, o) for a, o in near if lengths[a] >= 4]
    for axis, offset in first_round:
        greet(rounds.at[0], along(axis, offset))
    for z in range(1, depth_size - 1):
        look_up(z, 0)
        look_up(z, rows - 1)
    start_halo(2)
    start_halo(3)

    @pl.when(jnp.logical_not(has_before))
    def _():
        for y in range(rows):
            dens[0, y + 1] = zero

    @pl.when(jnp.logical_not(has_after))
    def _():
        for y in range(rows):
            dens[depth_size + 1, y + 1] = zero

    @pl.when(jnp.logical_not(has_down))
    def _():
        for z in range(depth_size):
            dens[z + 1, 0] = zero

    @pl.when(jnp.logical_not(has_up))
    def _():
        for z in range(depth_size):
            dens[z + 1, rows + 1] = zero

    def look_up_layer(z, carry):
        for y in range(1, rows - 1):
            look_up(z, y)
        return carry

    lax.fori_loop(1, depth_size - 1, look_up_layer, 0)

    rate = -2.0 / (255.0 * depth_size * groups)
    for y in range(rows):
        total = dens[1, y + 1]
        for z in range(1, depth_size):
            total = total + dens[z + 1, y + 1]
        send_pass[y] = jnp.exp(total * rate)

    if first_round:
        pl.semaphore_wait(rounds.at[0], len(first_round))
    second_round = [(a, o) for a, n in lengths.items() if n >= 8 for o in (2, n - 2)]
    for axis, offset in second_round:
        greet(rounds.at[1], along(axis, offset))
    if second_round:
        pl.semaphore_wait(rounds.at[1], len(second_round))
    third_round = [("x", o) for o in range(1, size_x)] if size_z > 1 else []
    for axis, offset in third_round:
        greet(rounds.at[2], along(axis, offset))

    def block_copy(sent, got, which, target):
        return pltpu.make_async_remote_copy(
            src_ref=sent.at[pl.ds(target * piece, piece)],
            dst_ref=got.at[me],
            send_sem=block_send.at[which],
            recv_sem=block_recv.at[which],
            device_id={"depth": target, "tile": tile},
            device_id_type=MESH,
        )

    def turn(step):
        half = (step + 1) // 2
        offset = groups // 2 + jnp.where(lax.rem(step, 2) == 0, half, -half)
        return lax.rem(me + offset + groups, groups)

    def pass_block(step, carry):
        block_copy(send_pass, got_pass, 0, turn(step)).start()
        return carry

    lax.fori_loop(0, groups - 1, pass_block, 0)

    for kind in range(4):

        @pl.when(arrives[kind])
        def _(kind=kind):
            halo(kind).wait_recv()

    def do_colour(step, carry):
        target = turn(step)
        for r in range(piece):
            y = target * piece + r
            total = zero
            through = one
            sums = [zero, zero, zero]
            for z in range(depth_size):
                word = words[z, y]
                value = dens[z + 1, y + 1]
                total = total + value
                after = jnp.exp(total * rate)
                right = pltpu.roll(value, LANES - 1, 1)
                right = jnp.where(last_lane, pltpu.roll(right, SUBLANES - 1, 0), right)
                right = jnp.where(last_cell, 0.0, right)
                left = pltpu.roll(value, 1, 1)
                left = jnp.where(first_lane, pltpu.roll(left, 1, 0), left)
                left = jnp.where(first_cell, 0.0, left)
                dz = dens[z + 2, y + 1] - dens[z, y + 1]
                dy = dens[z + 1, y + 2] - dens[z + 1, y]
                dx = right - left
                square = dz * dz + dy * dy + dx * dx
                toward = jnp.abs(
                    dz * (0.7 * LIGHT_Z) + dy * (0.7 * LIGHT_Y) + dx * (0.7 * LIGHT_X)
                )
                shade = 0.3 + toward * lax.rsqrt(jnp.maximum(square, (0.25 * 510.0) ** 2))
                weight = (through - after) * shade
                through = after
                for c in range(3):
                    part = lax.shift_right_logical(word, 8 * (c + 1))
                    if c < 2:
                        part = part & 255
                    sums[c] = sums[c] + part.astype(jnp.float32) * weight
            row = (tile * rows + y).astype(jnp.float32)
            ramp = (0.5 + (row + 0.5) / (rows * strips)) / 255.0
            for c in range(3):
                send_colour[y, c] = sums[c] * ramp

        @pl.when(target != me)
        def _():
            block_copy(send_colour, got_colour, 1, target).start()

        return carry

    lax.fori_loop(0, groups, do_colour, 0)

    for r in range(piece):
        got_pass[me, r] = send_pass[me * piece + r]
        for c in range(3):
            got_colour[me, r, c] = send_colour[me * piece + r, c]

    for rank in range(groups):
        at = 0
        for g in range(1, groups):
            at = jnp.where(order[0, g] == rank, g, at)
        inverse[rank] = at

    if third_round:
        pl.semaphore_wait(rounds.at[2], len(third_round))

    def all_but_one(ref, semaphore):
        part = ref.at[pl.ds(0, ref.shape[0] - 1)]
        return pltpu.make_async_copy(part, part, semaphore)

    all_but_one(got_pass, block_recv.at[0]).wait()
    all_but_one(got_colour, block_recv.at[1]).wait()

    composite = []
    ahead = []
    for r in range(piece):
        through = one
        sums = [zero, zero, zero]
        for rank in range(groups):
            g = inverse[rank]
            for c in range(3):
                sums[c] = sums[c] + through * got_colour[g, r, c]
            through = through * got_pass[g, r]
        composite.append(sums)
        ahead.append(through)

    logs = zero
    for r in range(piece):
        lum = 0.2126 * composite[r][0] + 0.7152 * composite[r][1] + 0.0722 * composite[r][2]
        logs = logs + jnp.log(0.05 + lum)
    local = jnp.sum(logs, axis=0, keepdims=True)

    def in_first(index):
        return {"depth": index // 2, "tile": chip * 2 + lax.rem(index, 2)}

    def in_second(index):
        return {"depth": me, "tile": index * 2 + core}

    stages = ((part_one, me * 2 + core, in_first), (part_two, chip, in_second))
    for stage, (parts, mine, device) in enumerate(stages):
        count = parts.shape[0]
        parts[mine] = local
        for offset in range(1, count):
            pltpu.make_async_remote_copy(
                src_ref=parts.at[mine],
                dst_ref=parts.at[mine],
                send_sem=sum_send.at[stage],
                recv_sem=sum_recv.at[stage],
                device_id=device(lax.rem(mine + offset, count)),
                device_id_type=MESH,
            ).start()
        all_but_one(parts, sum_recv.at[stage]).wait()
        local = jnp.sum(parts[...], axis=0)
    log_sum = jnp.sum(local, axis=1, keepdims=True)
    scale = KEY_VALUE / jnp.exp(log_sum * (1.0 / (rows * strips * cols)))
    scale = jnp.broadcast_to(scale, (SUBLANES, LANES))

    for r in range(piece):
        for c in range(3):
            scaled = composite[r][c] * scale
            frame_ref[c, :, r, :] = scaled / (1.0 + scaled)
        frame_ref[3, :, r, :] = 1.0 - ahead[r]

    for kind in range(4):

        @pl.when(sends[kind])
        def _(kind=kind):
            halo(kind).wait_send()

    all_but_one(got_pass, block_send.at[0]).wait()
    all_but_one(got_colour, block_send.at[1]).wait()
    all_but_one(part_one, sum_send.at[0]).wait()
    all_but_one(part_two, sum_send.at[1]).wait()


def body(labels, depth_order, opacity_table, colour_map):
    groups = lax.axis_size("depth")
    strips = lax.axis_size("tile")
    depth_size, rows, cols = labels.shape
    piece = rows // groups
    block = (SUBLANES, LANES)
    frame = pl.pallas_call(
        functools.partial(kernel, (groups, strips, depth_size, rows)),
        out_shape=pltpu.VMEM((4, SUBLANES, piece, LANES), jnp.float32),
        in_specs=[pl.BlockSpec(memory_space=pl.ANY)] * 4,
        out_specs=pl.BlockSpec(memory_space=pltpu.VMEM),
        scratch_shapes=[
            pltpu.VMEM((SUBLANES, depth_size, rows, LANES), jnp.int32),
            pltpu.SMEM((1, groups), jnp.int32),
            pltpu.VMEM((2 * LANES,), jnp.int32),
            pltpu.VMEM((3, 2 * LANES), jnp.int32),
            pltpu.VMEM((depth_size, rows) + block, jnp.int32),
            pltpu.VMEM((depth_size + 2, rows + 2) + block, jnp.float32),
            pltpu.VMEM((rows,) + block, jnp.float32),
            pltpu.VMEM((rows, 3) + block, jnp.float32),
            pltpu.VMEM((groups, piece) + block, jnp.float32),
            pltpu.VMEM((groups, piece, 3) + block, jnp.float32),
            pltpu.VMEM((groups * 2, 1, LANES), jnp.float32),
            pltpu.VMEM((strips // 2, 1, LANES), jnp.float32),
            pltpu.SMEM((groups,), jnp.int32),
            pltpu.SemaphoreType.DMA((4,)),
            pltpu.SemaphoreType.DMA((4,)),
            pltpu.SemaphoreType.DMA((4,)),
            pltpu.SemaphoreType.DMA((2,)),
            pltpu.SemaphoreType.DMA((2,)),
            pltpu.SemaphoreType.DMA((2,)),
            pltpu.SemaphoreType.DMA((2,)),
            pltpu.SemaphoreType.REGULAR((3,)),
        ],
        compiler_params=pltpu.CompilerParams(
            collective_id=0, has_side_effects=True, vmem_limit_bytes=32 * 1024 * 1024
        ),
        name="render",
    )(*[pltpu.with_memory_space_constraint(a, pltpu.HBM) for a in (labels, depth_order, opacity_table, colour_map)])
    return jnp.swapaxes(frame, 1, 2).reshape(4, 1, piece, cols)


def solution(mesh):
    in_specs = (P("depth", "tile", None), P("tile", None), P(), P())
    out_specs = P(None, "tile", "depth", None)
    return jax.shard_map(body, mesh=mesh, in_specs=in_specs, out_specs=out_specs, check_vma=False)
```

```python
import functools

import jax
import jax.numpy as jnp
from jax import lax
from jax.experimental import pallas as pl
from jax.experimental.pallas import tpu as pltpu
from jax.sharding import PartitionSpec as P

LIGHT_Z = 0.8
LIGHT_Y = 0.36
LIGHT_X = 0.48
KEY_VALUE = 0.18
SIZE_X = 4
LANES = 128
SUBLANES = 8
MESH = pl.DeviceIdType.MESH


def gathered(table, index):
    return jnp.take_along_axis(table, index, axis=1, mode="promise_in_bounds")


def image_row(labels, z, y):
    blocks, depth_size, rows, lanes = labels.shape
    flat = labels.reshape(blocks * depth_size * rows, lanes)
    return flat[pl.ds(z * rows + y, blocks, stride=depth_size * rows), :]


def kernel(
    sizes,
    labels_hbm,
    order_hbm,
    opacity_hbm,
    colour_hbm,
    frame_ref,
    labels,
    order,
    opacity,
    colour,
    words,
    dens,
    send_pass,
    send_colour,
    got_pass,
    got_colour,
    part_one,
    part_two,
    inverse,
    load_sem,
    halo_send,
    layer_recv,
    row_recv,
    block_send,
    block_recv,
    sum_send,
    sum_recv,
    rounds,
):
    groups, strips, depth_size, rows = sizes
    cols = SUBLANES * LANES
    piece = rows // groups
    size_x = min(SIZE_X, strips // 2)
    size_z = strips // (2 * size_x)
    me = lax.axis_index("depth")
    tile = lax.axis_index("tile")
    chip = tile >> 1
    core = tile & 1
    at_x = chip & (size_x - 1)
    at_z = lax.div(chip, size_x)
    lengths = {"y": groups, "x": size_x, "z": size_z}

    def along(axis, offset):
        if axis == "y":
            return {"depth": (me + offset) & (groups - 1), "tile": tile}
        if axis == "x":
            there = at_z * size_x + ((at_x + offset) & (size_x - 1))
        else:
            there = ((at_z + offset) & (size_z - 1)) * size_x + at_x
        return {"depth": me, "tile": there * 2 + core}

    def greet(semaphore, device):
        pl.semaphore_signal(semaphore, inc=1, device_id=device, device_id_type=MESH)

    barrier = pltpu.get_barrier_semaphore()
    has_up = tile < strips - 1
    has_down = tile > 0
    has_after = me < groups - 1
    has_before = me > 0
    other_core = {"depth": me, "tile": tile + 1 - 2 * core}
    near = [(a, o) for a, n in lengths.items() if n > 1 for o in sorted({1, n - 1})]
    for axis, offset in near:
        greet(barrier, along(axis, offset))
    greet(barrier, other_core)
    beside = jnp.where(core == 0, tile - 1, tile + 1)
    has_beside = (beside >= 0) & (beside < strips)
    beside_near = jnp.where(core == 0, at_x > 0, at_x < size_x - 1)
    beside_far = jnp.logical_and(has_beside, jnp.logical_not(beside_near))

    next_x = (at_x + 2 * core - 1) & (size_x - 1)
    across = {"depth": me, "tile": (at_z * size_x + next_x) * 2 + 1 - core}
    greet(barrier, across)

    for block in range(SUBLANES):
        pltpu.make_async_copy(
            labels_hbm.at[:, :, pl.ds(block * LANES, LANES)], labels.at[block], load_sem.at[0]
        ).start()
    loads = [
        pltpu.make_async_copy(opacity_hbm, opacity, load_sem.at[1]),
        pltpu.make_async_copy(colour_hbm, colour, load_sem.at[2]),
        pltpu.make_async_copy(order_hbm, order, load_sem.at[3]),
    ]
    for load in loads:
        load.start()
    for load in loads:
        load.wait()

    level = [opacity[...].reshape(1, 2 * LANES)] + [colour[c : c + 1, :] for c in range(3)]
    packed = level[0] + level[1] * 256 + level[2] * 65536 + level[3] * 16777216
    low = jnp.broadcast_to(packed[:, :LANES], (SUBLANES, LANES))
    high = jnp.broadcast_to(packed[:, LANES:], (SUBLANES, LANES))
    lane = lax.broadcasted_iota(jnp.int32, (SUBLANES, LANES), 1)
    sub = lax.broadcasted_iota(jnp.int32, (SUBLANES, LANES), 0)
    first_lane, last_lane = lane == 0, lane == LANES - 1
    first_cell = first_lane & (sub == 0)
    last_cell = last_lane & (sub == SUBLANES - 1)
    zero = jnp.zeros((SUBLANES, LANES), jnp.float32)
    one = jnp.ones((SUBLANES, LANES), jnp.float32)
    pltpu.make_async_copy(labels, labels, load_sem.at[0]).wait()

    def look_up(z, y):
        label = image_row(labels, z, y)
        index = label & (LANES - 1)
        word = jnp.where(label < LANES, gathered(low, index), gathered(high, index))
        words[z, y] = word
        dens[z + 1, y + 1] = (word & 255).astype(jnp.float32)

    def block_at(depth, step):
        inner = groups - 2
        turn = depth + groups // 2 - 1 + step
        for _ in range(2):
            turn = jnp.where(turn >= inner, turn - inner, turn)
        swap = (depth < groups // 2).astype(jnp.int32)
        last = jnp.where(step - inner == swap, 0, groups - 1)
        return jnp.where(step < inner, turn + 1, last)

    def start_layer(kind):
        target = me + 1 if kind == 0 else me - 1
        src, dst = (depth_size, 0) if kind == 0 else (1, depth_size + 1)
        for step in range(groups):
            part = pl.ds(block_at(target, step) * piece + 1, piece)
            pltpu.make_async_remote_copy(
                src_ref=dens.at[src, part],
                dst_ref=dens.at[dst, part],
                send_sem=halo_send.at[kind],
                recv_sem=layer_recv.at[kind, step // 2],
                device_id={"depth": target, "tile": tile},
                device_id_type=MESH,
            ).start()

    def rows_copy(count, semaphore):
        part = dens.at[0, pl.ds(0, count)]
        return pltpu.make_async_copy(part, part, semaphore)

    def row_copy(up):
        row, there = (rows, 0) if up else (1, rows + 1)
        return pltpu.make_async_remote_copy(
            src_ref=dens.at[pl.ds(1, depth_size), row],
            dst_ref=dens.at[pl.ds(1, depth_size), there],
            send_sem=halo_send.at[2 if up else 3],
            recv_sem=row_recv.at[0 if up else 1],
            device_id={"depth": me, "tile": tile + 1 if up else tile - 1},
            device_id_type=MESH,
        )

    def start_row(up, condition):
        @pl.when(condition)
        def _():
            row_copy(up).start()

    sends = (has_after, has_before, has_up, has_down)

    for y in range(rows):
        look_up(depth_size - 1, y)
        look_up(0, y)
    pl.semaphore_wait(barrier, len(near) + 2)

    @pl.when(has_after)
    def _():
        start_layer(0)

    @pl.when(has_before)
    def _():
        start_layer(1)

    first_round = [(a, o) for a, o in near if lengths[a] >= 4]
    for axis, offset in first_round:
        greet(rounds.at[0], along(axis, offset))
    if size_z > 1:
        greet(rounds.at[0], across)
    for z in range(1, depth_size - 1):
        look_up(z, 0)
        look_up(z, rows - 1)
    start_row(True, (core == 0) | beside_near)
    start_row(False, (core == 1) | beside_near)

    @pl.when(jnp.logical_not(has_before))
    def _():
        for y in range(rows):
            dens[0, y + 1] = zero

    @pl.when(jnp.logical_not(has_after))
    def _():
        for y in range(rows):
            dens[depth_size + 1, y + 1] = zero

    @pl.when(jnp.logical_not(has_down))
    def _():
        for z in range(depth_size):
            dens[z + 1, 0] = zero

    @pl.when(jnp.logical_not(has_up))
    def _():
        for z in range(depth_size):
            dens[z + 1, rows + 1] = zero

    def look_up_layer(z, carry):
        for y in range(1, rows - 1):
            look_up(z, y)
        return carry

    lax.fori_loop(1, depth_size - 1, look_up_layer, 0)

    rate = -2.0 / (255.0 * depth_size * groups)
    for y in range(rows):
        total = dens[1, y + 1]
        for z in range(1, depth_size):
            total = total + dens[z + 1, y + 1]
        send_pass[y] = jnp.exp(total * rate)

    def block_copy(sent, got, which, target):
        return pltpu.make_async_remote_copy(
            src_ref=sent.at[pl.ds(target * piece, piece)],
            dst_ref=got.at[me],
            send_sem=block_send.at[which],
            recv_sem=block_recv.at[which],
            device_id={"depth": target, "tile": tile},
            device_id_type=MESH,
        )

    def send_passes(offsets):
        for offset in offsets:
            block_copy(send_pass, got_pass, 0, (me + offset) & (groups - 1)).start()

    pl.semaphore_wait(rounds.at[0], len(first_round) + (size_z > 1))
    second_round = [(a, o) for a, n in lengths.items() if n >= 8 for o in (2, n - 2)]
    for axis, offset in second_round:
        greet(rounds.at[1], along(axis, offset))
    start_row(True, (core == 1) & beside_far)
    start_row(False, (core == 0) & beside_far)
    send_passes((2, groups - 2, 1, groups - 1))
    if second_round:
        pl.semaphore_wait(rounds.at[1], len(second_round))
    third_round = [("x", o) for o in range(1, size_x)] if size_z > 1 else []
    for axis, offset in third_round:
        greet(rounds.at[2], along(axis, offset))
    send_passes(range(3, groups - 2))

    def do_colour(target):
        for r in range(piece):
            y = target * piece + r
            total = zero
            through = one
            sums = [zero, zero, zero]
            for z in range(depth_size):
                word = words[z, y]
                value = dens[z + 1, y + 1]
                total = total + value
                after = jnp.exp(total * rate)
                right = pltpu.roll(value, LANES - 1, 1)
                right = jnp.where(last_lane, pltpu.roll(right, SUBLANES - 1, 0), right)
                right = jnp.where(last_cell, 0.0, right)
                left = pltpu.roll(value, 1, 1)
                left = jnp.where(first_lane, pltpu.roll(left, 1, 0), left)
                left = jnp.where(first_cell, 0.0, left)
                dz = dens[z + 2, y + 1] - dens[z, y + 1]
                dy = dens[z + 1, y + 2] - dens[z + 1, y]
                dx = right - left
                square = dz * dz + dy * dy + dx * dx
                toward = jnp.abs(
                    dz * (0.7 * LIGHT_Z) + dy * (0.7 * LIGHT_Y) + dx * (0.7 * LIGHT_X)
                )
                shade = 0.3 + toward * lax.rsqrt(jnp.maximum(square, (0.25 * 510.0) ** 2))
                weight = (through - after) * shade
                through = after
                for c in range(3):
                    part = lax.shift_right_logical(word, 8 * (c + 1))
                    if c < 2:
                        part = part & 255
                    sums[c] = sums[c] + part.astype(jnp.float32) * weight
            row = (tile * rows + y).astype(jnp.float32)
            ramp = (0.5 + (row + 0.5) / (rows * strips)) / 255.0
            for c in range(3):
                send_colour[y, c] = sums[c] * ramp

        @pl.when(target != me)
        def _():
            block_copy(send_colour, got_colour, 1, target).start()

    def colour_pair(pair, carry):
        for kind, arrives in enumerate((has_before, has_after)):

            @pl.when(arrives)
            def _(kind=kind):
                rows_copy(2 * piece, layer_recv.at[kind, pair]).wait()

        @pl.when((pair == groups // 2 - 1) & has_down)
        def _():
            row_copy(True).wait_recv()

        @pl.when((pair == groups // 2 - 1) & has_up)
        def _():
            row_copy(False).wait_recv()

        def step(half, carry):
            do_colour(block_at(me, pair * 2 + half))
            return carry

        return lax.fori_loop(0, 2, step, carry)

    lax.fori_loop(0, groups // 2, colour_pair, 0)

    for r in range(piece):
        got_pass[me, r] = send_pass[me * piece + r]
        for c in range(3):
            got_colour[me, r, c] = send_colour[me * piece + r, c]

    for rank in range(groups):
        at = 0
        for g in range(1, groups):
            at = jnp.where(order[0, g] == rank, g, at)
        inverse[rank] = at

    if third_round:
        pl.semaphore_wait(rounds.at[2], len(third_round))

    def all_but_one(ref, semaphore):
        part = ref.at[pl.ds(0, ref.shape[0] - 1)]
        return pltpu.make_async_copy(part, part, semaphore)

    all_but_one(got_pass, block_recv.at[0]).wait()
    all_but_one(got_colour, block_recv.at[1]).wait()

    composite = []
    ahead = []
    for r in range(piece):
        through = one
        sums = [zero, zero, zero]
        for rank in range(groups):
            g = inverse[rank]
            for c in range(3):
                sums[c] = sums[c] + through * got_colour[g, r, c]
            through = through * got_pass[g, r]
        composite.append(sums)
        ahead.append(through)

    logs = zero
    for r in range(piece):
        lum = 0.2126 * composite[r][0] + 0.7152 * composite[r][1] + 0.0722 * composite[r][2]
        logs = logs + jnp.log(0.05 + lum)
    local = jnp.sum(logs, axis=0, keepdims=True)

    def in_first(index):
        return {"depth": index >> 1, "tile": chip * 2 + (index & 1)}

    def in_second(index):
        return {"depth": me, "tile": index * 2 + core}

    stages = ((part_one, me * 2 + core, in_first), (part_two, chip, in_second))
    for stage, (parts, mine, device) in enumerate(stages):
        count = parts.shape[0]
        parts[mine] = local
        for offset in range(1, count):
            pltpu.make_async_remote_copy(
                src_ref=parts.at[mine],
                dst_ref=parts.at[mine],
                send_sem=sum_send.at[stage],
                recv_sem=sum_recv.at[stage],
                device_id=device((mine + offset) & (count - 1)),
                device_id_type=MESH,
            ).start()
        all_but_one(parts, sum_recv.at[stage]).wait()
        local = jnp.sum(parts[...], axis=0)
    log_sum = jnp.sum(local, axis=1, keepdims=True)
    scale = KEY_VALUE / jnp.exp(log_sum * (1.0 / (rows * strips * cols)))
    scale = jnp.broadcast_to(scale, (SUBLANES, LANES))

    for r in range(piece):
        for c in range(3):
            scaled = composite[r][c] * scale
            frame_ref[c, :, r, :] = scaled / (1.0 + scaled)
        frame_ref[3, :, r, :] = 1.0 - ahead[r]

    for kind in range(4):

        @pl.when(sends[kind])
        def _(kind=kind):
            rows_copy(rows if kind < 2 else depth_size, halo_send.at[kind]).wait()

    all_but_one(got_pass, block_send.at[0]).wait()
    all_but_one(got_colour, block_send.at[1]).wait()
    all_but_one(part_one, sum_send.at[0]).wait()
    all_but_one(part_two, sum_send.at[1]).wait()


def body(labels, depth_order, opacity_table, colour_map):
    groups = lax.axis_size("depth")
    strips = lax.axis_size("tile")
    depth_size, rows, cols = labels.shape
    piece = rows // groups
    block = (SUBLANES, LANES)
    frame = pl.pallas_call(
        functools.partial(kernel, (groups, strips, depth_size, rows)),
        out_shape=pltpu.VMEM((4, SUBLANES, piece, LANES), jnp.float32),
        in_specs=[pl.BlockSpec(memory_space=pl.ANY)] * 4,
        out_specs=pl.BlockSpec(memory_space=pltpu.VMEM),
        scratch_shapes=[
            pltpu.VMEM((SUBLANES, depth_size, rows, LANES), jnp.int32),
            pltpu.SMEM((1, groups), jnp.int32),
            pltpu.VMEM((2 * LANES,), jnp.int32),
            pltpu.VMEM((3, 2 * LANES), jnp.int32),
            pltpu.VMEM((depth_size, rows) + block, jnp.int32),
            pltpu.VMEM((depth_size + 2, rows + 2) + block, jnp.float32),
            pltpu.VMEM((rows,) + block, jnp.float32),
            pltpu.VMEM((rows, 3) + block, jnp.float32),
            pltpu.VMEM((groups, piece) + block, jnp.float32),
            pltpu.VMEM((groups, piece, 3) + block, jnp.float32),
            pltpu.VMEM((groups * 2, 1, LANES), jnp.float32),
            pltpu.VMEM((strips // 2, 1, LANES), jnp.float32),
            pltpu.SMEM((groups,), jnp.int32),
            pltpu.SemaphoreType.DMA((4,)),
            pltpu.SemaphoreType.DMA((4,)),
            pltpu.SemaphoreType.DMA((2, groups // 2)),
            pltpu.SemaphoreType.DMA((2,)),
            pltpu.SemaphoreType.DMA((2,)),
            pltpu.SemaphoreType.DMA((2,)),
            pltpu.SemaphoreType.DMA((2,)),
            pltpu.SemaphoreType.DMA((2,)),
            pltpu.SemaphoreType.REGULAR((3,)),
        ],
        compiler_params=pltpu.CompilerParams(
            collective_id=0, has_side_effects=True, vmem_limit_bytes=32 * 1024 * 1024
        ),
        name="render",
    )(*[pltpu.with_memory_space_constraint(a, pltpu.HBM) for a in (labels, depth_order, opacity_table, colour_map)])
    return jnp.swapaxes(frame, 1, 2).reshape(4, 1, piece, cols)


def solution(mesh):
    in_specs = (P("depth", "tile", None), P("tile", None), P(), P())
    out_specs = P(None, "tile", "depth", None)
    return jax.shard_map(body, mesh=mesh, in_specs=in_specs, out_specs=out_specs, check_vma=False)
```

```python
import functools

import jax
import jax.numpy as jnp
from jax import lax
from jax.experimental import pallas as pl
from jax.experimental.pallas import tpu as pltpu
from jax.sharding import PartitionSpec as P

LIGHT_Z = 0.8
LIGHT_Y = 0.36
LIGHT_X = 0.48
KEY_VALUE = 0.18
SIZE_X = 4
LANES = 128
SUBLANES = 8
MESH = pl.DeviceIdType.MESH


def gathered(table, index):
    return jnp.take_along_axis(table, index, axis=1, mode="promise_in_bounds")


def image_row(labels, z, y):
    blocks, depth_size, rows, lanes = labels.shape
    flat = labels.reshape(blocks * depth_size * rows, lanes)
    return flat[pl.ds(z * rows + y, blocks, stride=depth_size * rows), :]


def kernel(
    sizes,
    labels_hbm,
    order_hbm,
    opacity_hbm,
    colour_hbm,
    frame_ref,
    labels,
    order,
    opacity,
    colour,
    words,
    dens,
    send_pass,
    send_colour,
    got_pass,
    got_colour,
    part_one,
    part_two,
    inverse,
    load_sem,
    halo_send,
    layer_recv,
    row_recv,
    block_send,
    block_recv,
    sum_send,
    sum_recv,
    rounds,
):
    groups, strips, depth_size, rows = sizes
    cols = SUBLANES * LANES
    piece = rows // groups
    size_x = min(SIZE_X, strips // 2)
    size_z = strips // (2 * size_x)
    me = lax.axis_index("depth")
    tile = lax.axis_index("tile")
    chip = tile >> 1
    core = tile & 1
    at_x = chip & (size_x - 1)
    at_z = lax.div(chip, size_x)
    lengths = {"y": groups, "x": size_x, "z": size_z}

    def along(axis, offset):
        if axis == "y":
            return {"depth": (me + offset) & (groups - 1), "tile": tile}
        if axis == "x":
            there = at_z * size_x + ((at_x + offset) & (size_x - 1))
        else:
            there = ((at_z + offset) & (size_z - 1)) * size_x + at_x
        return {"depth": me, "tile": there * 2 + core}

    def greet(semaphore, device):
        pl.semaphore_signal(semaphore, inc=1, device_id=device, device_id_type=MESH)

    barrier = pltpu.get_barrier_semaphore()
    has_up = tile < strips - 1
    has_down = tile > 0
    has_after = me < groups - 1
    has_before = me > 0
    ring = sorted(range(1, groups), key=lambda offset: -min(offset, groups - offset))
    near = [(a, o) for a in ("x", "z") if lengths[a] > 1 for o in sorted({1, lengths[a] - 1})]

    tuned = groups == 8

    def told_later(source, target):
        if not tuned:
            return jnp.bool_(False)
        late = ((source == 4) & (target < 3)) | ((source == 5) & (target < 4))
        return late | ((source == 7) & (target == 3))

    def tells(source, target):
        late = ((source == 4) & (target < 3)) | ((source == 5) & (target < 4))
        return late | ((source == 0) & (target == 3))

    for offset in ring:

        @pl.when(jnp.logical_not(told_later(me, (me + offset) & (groups - 1))))
        def _(offset=offset):
            greet(barrier, along("y", offset))

    @pl.when(has_up)
    def _():
        greet(barrier, {"depth": me, "tile": tile + 1})

    @pl.when(has_down)
    def _():
        greet(barrier, {"depth": me, "tile": tile - 1})

    for axis, offset in near:
        greet(barrier, along(axis, offset))
    tidings = jnp.where(me < 4, 2, 0) if tuned else 0
    greeted = len(ring) - tidings + len(near) + has_up.astype(jnp.int32) + has_down.astype(jnp.int32)

    for block in range(SUBLANES):
        pltpu.make_async_copy(
            labels_hbm.at[:, :, pl.ds(block * LANES, LANES)], labels.at[block], load_sem.at[0]
        ).start()
    loads = [
        pltpu.make_async_copy(opacity_hbm, opacity, load_sem.at[1]),
        pltpu.make_async_copy(colour_hbm, colour, load_sem.at[2]),
        pltpu.make_async_copy(order_hbm, order, load_sem.at[3]),
    ]
    for load in loads:
        load.start()
    for load in loads:
        load.wait()

    level = [opacity[...].reshape(1, 2 * LANES)] + [colour[c : c + 1, :] for c in range(3)]
    packed = level[0] + level[1] * 256 + level[2] * 65536 + level[3] * 16777216
    low = jnp.broadcast_to(packed[:, :LANES], (SUBLANES, LANES))
    high = jnp.broadcast_to(packed[:, LANES:], (SUBLANES, LANES))
    lane = lax.broadcasted_iota(jnp.int32, (SUBLANES, LANES), 1)
    sub = lax.broadcasted_iota(jnp.int32, (SUBLANES, LANES), 0)
    first_lane, last_lane = lane == 0, lane == LANES - 1
    first_cell = first_lane & (sub == 0)
    last_cell = last_lane & (sub == SUBLANES - 1)
    zero = jnp.zeros((SUBLANES, LANES), jnp.float32)
    one = jnp.ones((SUBLANES, LANES), jnp.float32)
    pltpu.make_async_copy(labels, labels, load_sem.at[0]).wait()

    def look_up(z, y):
        label = image_row(labels, z, y)
        index = label & (LANES - 1)
        word = jnp.where(label < LANES, gathered(low, index), gathered(high, index))
        words[z, y] = word
        dens[z + 1, y + 1] = (word & 255).astype(jnp.float32)

    def block_at(depth, step):
        third = (groups - 2) // 2
        turn = lax.rem(depth + step + 1, third)
        middle = turn + (groups - third + 1) // 2
        outer = jnp.where(turn < third // 2 + 1, turn + 1, turn + third + 1)
        ends = jnp.where(step - (groups - 2) == (depth < groups // 2).astype(jnp.int32), 0, groups - 1)
        return jnp.where(step < third, middle, jnp.where(step < 2 * third, outer, ends))

    def start_layer(kind):
        target = me + 1 if kind == 0 else me - 1
        src, dst = (depth_size, 0) if kind == 0 else (1, depth_size + 1)
        for step in range(groups):
            part = pl.ds(block_at(target, step) * piece + 1, piece)
            pltpu.make_async_remote_copy(
                src_ref=dens.at[src, part],
                dst_ref=dens.at[dst, part],
                send_sem=halo_send.at[kind],
                recv_sem=layer_recv.at[kind, step // 2],
                device_id={"depth": target, "tile": tile},
                device_id_type=MESH,
            ).start()

    def rows_copy(count, semaphore):
        part = dens.at[0, pl.ds(0, count)]
        return pltpu.make_async_copy(part, part, semaphore)

    def row_copy(up):
        row, there = (rows, 0) if up else (1, rows + 1)
        return pltpu.make_async_remote_copy(
            src_ref=dens.at[pl.ds(1, depth_size), row],
            dst_ref=dens.at[pl.ds(1, depth_size), there],
            send_sem=halo_send.at[2 if up else 3],
            recv_sem=row_recv.at[0 if up else 1],
            device_id={"depth": me, "tile": tile + 1 if up else tile - 1},
            device_id_type=MESH,
        )

    def start_row(up):
        @pl.when(has_up if up else has_down)
        def _():
            row_copy(up).start()

    sends = (has_after, has_before, has_up, has_down)

    for y in range(rows):
        look_up(depth_size - 1, y)
        look_up(0, y)
    pl.semaphore_wait(barrier, greeted)
    for offset in ring if tuned else ():

        @pl.when(tells(me, (me + offset) & (groups - 1)))
        def _(offset=offset):
            greet(rounds.at[3], along("y", offset))


    @pl.when(has_after)
    def _():
        start_layer(0)

    @pl.when(has_before)
    def _():
        start_layer(1)

    for axis, offset in near:
        greet(rounds.at[0], along(axis, offset))
    for z in range(1, depth_size - 1):
        look_up(z, 0)
        look_up(z, rows - 1)
    start_row(True)
    start_row(False)

    @pl.when(jnp.logical_not(has_before))
    def _():
        for y in range(rows):
            dens[0, y + 1] = zero

    @pl.when(jnp.logical_not(has_after))
    def _():
        for y in range(rows):
            dens[depth_size + 1, y + 1] = zero

    @pl.when(jnp.logical_not(has_down))
    def _():
        for z in range(depth_size):
            dens[z + 1, 0] = zero

    @pl.when(jnp.logical_not(has_up))
    def _():
        for z in range(depth_size):
            dens[z + 1, rows + 1] = zero

    def look_up_layer(z, carry):
        for y in range(1, rows - 1):
            look_up(z, y)
        return carry

    lax.fori_loop(1, depth_size - 1, look_up_layer, 0)

    rate = -2.0 / (255.0 * depth_size * groups)
    for y in range(rows):
        total = dens[1, y + 1]
        for z in range(1, depth_size):
            total = total + dens[z + 1, y + 1]
        send_pass[y] = jnp.exp(total * rate)

    def block_copy(sent, got, which, target):
        return pltpu.make_async_remote_copy(
            src_ref=sent.at[pl.ds(target * piece, piece)],
            dst_ref=got.at[me],
            send_sem=block_send.at[which],
            recv_sem=block_recv.at[which],
            device_id={"depth": target, "tile": tile},
            device_id_type=MESH,
        )

    if tuned:

        @pl.when(me < 4)
        def _():
            pl.semaphore_wait(rounds.at[3], 2)

    for offset in ring:
        block_copy(send_pass, got_pass, 0, (me + offset) & (groups - 1)).start()

    def do_colour(target):
        for r in range(piece):
            y = target * piece + r
            total = zero
            through = one
            sums = [zero, zero, zero]
            for z in range(depth_size):
                word = words[z, y]
                value = dens[z + 1, y + 1]
                total = total + value
                after = jnp.exp(total * rate)
                right = pltpu.roll(value, LANES - 1, 1)
                right = jnp.where(last_lane, pltpu.roll(right, SUBLANES - 1, 0), right)
                right = jnp.where(last_cell, 0.0, right)
                left = pltpu.roll(value, 1, 1)
                left = jnp.where(first_lane, pltpu.roll(left, 1, 0), left)
                left = jnp.where(first_cell, 0.0, left)
                dz = dens[z + 2, y + 1] - dens[z, y + 1]
                dy = dens[z + 1, y + 2] - dens[z + 1, y]
                dx = right - left
                square = dz * dz + dy * dy + dx * dx
                toward = jnp.abs(
                    dz * (0.7 * LIGHT_Z) + dy * (0.7 * LIGHT_Y) + dx * (0.7 * LIGHT_X)
                )
                shade = 0.3 + toward * lax.rsqrt(jnp.maximum(square, (0.25 * 510.0) ** 2))
                weight = (through - after) * shade
                through = after
                for c in range(3):
                    part = lax.shift_right_logical(word, 8 * (c + 1))
                    if c < 2:
                        part = part & 255
                    sums[c] = sums[c] + part.astype(jnp.float32) * weight
            row = (tile * rows + y).astype(jnp.float32)
            ramp = (0.5 + (row + 0.5) / (rows * strips)) / 255.0
            for c in range(3):
                send_colour[y, c] = sums[c] * ramp

        @pl.when(target != me)
        def _():
            block_copy(send_colour, got_colour, 1, target).start()

    def colour_pair(pair, carry):
        for kind, arrives in enumerate((has_before, has_after)):

            @pl.when(arrives)
            def _(kind=kind):
                rows_copy(2 * piece, layer_recv.at[kind, pair]).wait()

        @pl.when((pair == groups // 2 - 1) & has_down)
        def _():
            row_copy(True).wait_recv()

        @pl.when((pair == groups // 2 - 1) & has_up)
        def _():
            row_copy(False).wait_recv()

        def step(half, carry):
            do_colour(block_at(me, pair * 2 + half))
            return carry

        return lax.fori_loop(0, 2, step, carry)

    lax.fori_loop(0, groups // 2, colour_pair, 0)

    for r in range(piece):
        got_pass[me, r] = send_pass[me * piece + r]
        for c in range(3):
            got_colour[me, r, c] = send_colour[me * piece + r, c]

    for rank in range(groups):
        at = 0
        for g in range(1, groups):
            at = jnp.where(order[0, g] == rank, g, at)
        inverse[rank] = at

    if near:
        pl.semaphore_wait(rounds.at[0], len(near))
    second_round = [("z", o) for o in (2, size_z - 2) if size_z >= 8]
    for axis, offset in second_round:
        greet(rounds.at[1], along(axis, offset))
    if second_round:
        pl.semaphore_wait(rounds.at[1], len(second_round))
    third_round = [("x", o) for o in range(1, size_x) if size_z > 1]
    for axis, offset in third_round:
        greet(rounds.at[2], along(axis, offset))

    def all_but_one(ref, semaphore):
        part = ref.at[pl.ds(0, ref.shape[0] - 1)]
        return pltpu.make_async_copy(part, part, semaphore)

    all_but_one(got_pass, block_recv.at[0]).wait()
    all_but_one(got_colour, block_recv.at[1]).wait()

    composite = []
    ahead = []
    for r in range(piece):
        through = one
        sums = [zero, zero, zero]
        for rank in range(groups):
            g = inverse[rank]
            for c in range(3):
                sums[c] = sums[c] + through * got_colour[g, r, c]
            through = through * got_pass[g, r]
        composite.append(sums)
        ahead.append(through)

    logs = zero
    for r in range(piece):
        lum = 0.2126 * composite[r][0] + 0.7152 * composite[r][1] + 0.0722 * composite[r][2]
        logs = logs + jnp.log(0.05 + lum)
    local = jnp.sum(logs, axis=0, keepdims=True)

    def in_first(index):
        return {"depth": index >> 1, "tile": chip * 2 + (index & 1)}

    def in_second(index):
        return {"depth": me, "tile": index * 2 + core}

    stages = ((part_one, me * 2 + core, in_first), (part_two, chip, in_second))
    for stage, (parts, mine, device) in enumerate(stages):
        count = parts.shape[0]
        parts[mine] = local
        if stage == 1 and third_round:
            pl.semaphore_wait(rounds.at[2], len(third_round))
        for offset in range(1, count):
            pltpu.make_async_remote_copy(
                src_ref=parts.at[mine],
                dst_ref=parts.at[mine],
                send_sem=sum_send.at[stage],
                recv_sem=sum_recv.at[stage],
                device_id=device((mine + offset) & (count - 1)),
                device_id_type=MESH,
            ).start()
        all_but_one(parts, sum_recv.at[stage]).wait()
        local = jnp.sum(parts[...], axis=0)
    log_sum = jnp.sum(local, axis=1, keepdims=True)
    scale = KEY_VALUE / jnp.exp(log_sum * (1.0 / (rows * strips * cols)))
    scale = jnp.broadcast_to(scale, (SUBLANES, LANES))

    for r in range(piece):
        for c in range(3):
            scaled = composite[r][c] * scale
            frame_ref[c, :, r, :] = scaled / (1.0 + scaled)
        frame_ref[3, :, r, :] = 1.0 - ahead[r]

    for kind in range(4):

        @pl.when(sends[kind])
        def _(kind=kind):
            rows_copy(rows if kind < 2 else depth_size, halo_send.at[kind]).wait()

    all_but_one(got_pass, block_send.at[0]).wait()
    all_but_one(got_colour, block_send.at[1]).wait()
    all_but_one(part_one, sum_send.at[0]).wait()
    all_but_one(part_two, sum_send.at[1]).wait()


def body(labels, depth_order, opacity_table, colour_map):
    groups = lax.axis_size("depth")
    strips = lax.axis_size("tile")
    depth_size, rows, cols = labels.shape
    piece = rows // groups
    block = (SUBLANES, LANES)
    frame = pl.pallas_call(
        functools.partial(kernel, (groups, strips, depth_size, rows)),
        out_shape=pltpu.VMEM((4, SUBLANES, piece, LANES), jnp.float32),
        in_specs=[pl.BlockSpec(memory_space=pl.ANY)] * 4,
        out_specs=pl.BlockSpec(memory_space=pltpu.VMEM),
        scratch_shapes=[
            pltpu.VMEM((SUBLANES, depth_size, rows, LANES), jnp.int32),
            pltpu.SMEM((1, groups), jnp.int32),
            pltpu.VMEM((2 * LANES,), jnp.int32),
            pltpu.VMEM((3, 2 * LANES), jnp.int32),
            pltpu.VMEM((depth_size, rows) + block, jnp.int32),
            pltpu.VMEM((depth_size + 2, rows + 2) + block, jnp.float32),
            pltpu.VMEM((rows,) + block, jnp.float32),
            pltpu.VMEM((rows, 3) + block, jnp.float32),
            pltpu.VMEM((groups, piece) + block, jnp.float32),
            pltpu.VMEM((groups, piece, 3) + block, jnp.float32),
            pltpu.VMEM((groups * 2, 1, LANES), jnp.float32),
            pltpu.VMEM((strips // 2, 1, LANES), jnp.float32),
            pltpu.SMEM((groups,), jnp.int32),
            pltpu.SemaphoreType.DMA((4,)),
            pltpu.SemaphoreType.DMA((4,)),
            pltpu.SemaphoreType.DMA((2, groups // 2)),
            pltpu.SemaphoreType.DMA((2,)),
            pltpu.SemaphoreType.DMA((2,)),
            pltpu.SemaphoreType.DMA((2,)),
            pltpu.SemaphoreType.DMA((2,)),
            pltpu.SemaphoreType.DMA((2,)),
            pltpu.SemaphoreType.REGULAR((4,)),
        ],
        compiler_params=pltpu.CompilerParams(
            collective_id=0, has_side_effects=True, vmem_limit_bytes=32 * 1024 * 1024
        ),
        name="render",
    )(*[pltpu.with_memory_space_constraint(a, pltpu.HBM) for a in (labels, depth_order, opacity_table, colour_map)])
    return jnp.swapaxes(frame, 1, 2).reshape(4, 1, piece, cols)


def solution(mesh):
    in_specs = (P("depth", "tile", None), P("tile", None), P(), P())
    out_specs = P(None, "tile", "depth", None)
    return jax.shard_map(body, mesh=mesh, in_specs=in_specs, out_specs=out_specs, check_vma=False)
```

```python
import functools
import math

import jax
import jax.numpy as jnp
from jax import lax
from jax.experimental import pallas as pl
from jax.experimental.pallas import tpu as pltpu
from jax.sharding import PartitionSpec as P

LIGHT_Z = 0.8
LIGHT_Y = 0.36
LIGHT_X = 0.48
KEY_VALUE = 0.18
SIZE_X = 4
LANES = 128
SUBLANES = 8
MESH = pl.DeviceIdType.MESH


def gathered(table, index):
    return jnp.take_along_axis(table, index, axis=1, mode="promise_in_bounds")


def image_row(labels, z, y):
    blocks, depth_size, rows, lanes = labels.shape
    flat = labels.reshape(blocks * depth_size * rows, lanes)
    return flat[pl.ds(z * rows + y, blocks, stride=depth_size * rows), :]


def kernel(
    sizes,
    labels_hbm,
    order_hbm,
    opacity_hbm,
    colour_hbm,
    frame_ref,
    labels,
    order,
    opacity,
    colour,
    words,
    dens,
    send_pass,
    send_colour,
    got_pass,
    got_colour,
    part_one,
    part_two,
    load_sem,
    halo_send,
    layer_recv,
    row_recv,
    block_send,
    block_recv,
    sum_send,
    sum_recv,
    rounds,
):
    groups, strips, depth_size, rows = sizes
    cols = SUBLANES * LANES
    piece = rows // groups
    size_x = min(SIZE_X, strips // 2)
    size_z = strips // (2 * size_x)
    me = lax.axis_index("depth")
    tile = lax.axis_index("tile")
    chip = tile >> 1
    core = tile & 1
    at_x = chip & (size_x - 1)
    at_z = lax.div(chip, size_x)
    lengths = {"y": groups, "x": size_x, "z": size_z}

    def along(axis, offset):
        if axis == "y":
            return {"depth": (me + offset) & (groups - 1), "tile": tile}
        if axis == "x":
            there = at_z * size_x + ((at_x + offset) & (size_x - 1))
        else:
            there = ((at_z + offset) & (size_z - 1)) * size_x + at_x
        return {"depth": me, "tile": there * 2 + core}

    def greet(semaphore, device):
        pl.semaphore_signal(semaphore, inc=1, device_id=device, device_id_type=MESH)

    barrier = pltpu.get_barrier_semaphore()
    has_up = tile < strips - 1
    has_down = tile > 0
    has_after = me < groups - 1
    has_before = me > 0
    ring = sorted(range(1, groups), key=lambda offset: -min(offset, groups - offset))
    near = [(a, o) for a in ("x", "z") if lengths[a] > 1 for o in sorted({1, lengths[a] - 1})]

    tuned = groups == 8

    def told_later(source, target):
        if not tuned:
            return jnp.bool_(False)
        late = ((source == 4) & (target < 3)) | ((source == 5) & (target < 4))
        return late | ((source == 7) & (target == 3))

    def tells(source, target):
        late = ((source == 4) & (target < 3)) | ((source == 5) & (target < 4))
        return late | ((source == 0) & (target == 3))

    for offset in ring:

        @pl.when(jnp.logical_not(told_later(me, (me + offset) & (groups - 1))))
        def _(offset=offset):
            greet(barrier, along("y", offset))

    @pl.when(has_up)
    def _():
        greet(barrier, {"depth": me, "tile": tile + 1})

    @pl.when(has_down)
    def _():
        greet(barrier, {"depth": me, "tile": tile - 1})

    for axis, offset in near:
        greet(barrier, along(axis, offset))
    tidings = jnp.where(me < 4, 2, 0) if tuned else 0
    greeted = len(ring) - tidings + len(near) + has_up.astype(jnp.int32) + has_down.astype(jnp.int32)

    for block in range(SUBLANES):
        pltpu.make_async_copy(
            labels_hbm.at[:, :, pl.ds(block * LANES, LANES)], labels.at[block], load_sem.at[0]
        ).start()
    loads = [
        pltpu.make_async_copy(opacity_hbm, opacity, load_sem.at[1]),
        pltpu.make_async_copy(colour_hbm, colour, load_sem.at[2]),
        pltpu.make_async_copy(order_hbm, order, load_sem.at[3]),
    ]
    for load in loads:
        load.start()
    for load in loads:
        load.wait()

    level = [opacity[...].reshape(1, 2 * LANES)] + [colour[c : c + 1, :] for c in range(3)]
    packed = level[0] + level[1] * 256 + level[2] * 65536 + level[3] * 16777216
    low = jnp.broadcast_to(packed[:, :LANES], (SUBLANES, LANES))
    high = jnp.broadcast_to(packed[:, LANES:], (SUBLANES, LANES))
    lane = lax.broadcasted_iota(jnp.int32, (SUBLANES, LANES), 1)
    sub = lax.broadcasted_iota(jnp.int32, (SUBLANES, LANES), 0)
    first_lane, last_lane = lane == 0, lane == LANES - 1
    first_cell = first_lane & (sub == 0)
    last_cell = last_lane & (sub == SUBLANES - 1)
    zero = jnp.zeros((SUBLANES, LANES), jnp.float32)
    one = jnp.ones((SUBLANES, LANES), jnp.float32)
    pltpu.make_async_copy(labels, labels, load_sem.at[0]).wait()

    def look_up(z, y):
        label = image_row(labels, z, y)
        index = label & (LANES - 1)
        word = jnp.where(label < LANES, gathered(low, index), gathered(high, index))
        words[z, y] = word
        dens[z + 1, y + 1] = (word & 255).astype(jnp.float32)

    def block_at(depth, step):
        third = (groups - 2) // 2
        turn = lax.rem(depth + step + 1, third)
        middle = turn + (groups - third + 1) // 2
        outer = jnp.where(turn < third // 2 + 1, turn + 1, turn + third + 1)
        ends = jnp.where(step - (groups - 2) == (depth < groups // 2).astype(jnp.int32), 0, groups - 1)
        return jnp.where(step < third, middle, jnp.where(step < 2 * third, outer, ends))

    def start_layer(kind):
        target = me + 1 if kind == 0 else me - 1
        src, dst = (depth_size, 0) if kind == 0 else (1, depth_size + 1)
        for step in range(groups):
            part = pl.ds(block_at(target, step) * piece + 1, piece)
            pltpu.make_async_remote_copy(
                src_ref=dens.at[src, part],
                dst_ref=dens.at[dst, part],
                send_sem=halo_send.at[kind],
                recv_sem=layer_recv.at[kind, step // 2],
                device_id={"depth": target, "tile": tile},
                device_id_type=MESH,
            ).start()

    def rows_copy(count, semaphore):
        part = dens.at[0, pl.ds(0, count)]
        return pltpu.make_async_copy(part, part, semaphore)

    def row_copy(up):
        row, there = (rows, 0) if up else (1, rows + 1)
        return pltpu.make_async_remote_copy(
            src_ref=dens.at[pl.ds(1, depth_size), row],
            dst_ref=dens.at[pl.ds(1, depth_size), there],
            send_sem=halo_send.at[2 if up else 3],
            recv_sem=row_recv.at[0 if up else 1],
            device_id={"depth": me, "tile": tile + 1 if up else tile - 1},
            device_id_type=MESH,
        )

    def start_row(up):
        @pl.when(has_up if up else has_down)
        def _():
            row_copy(up).start()

    sends = (has_after, has_before, has_up, has_down)

    def look_up_ends(row, carry):
        for y in range(4):
            look_up(depth_size - 1, row * 4 + y)
            look_up(0, row * 4 + y)
        return carry

    lax.fori_loop(0, rows // 4, look_up_ends, 0)
    pl.semaphore_wait(barrier, greeted)
    for offset in ring if tuned else ():

        @pl.when(tells(me, (me + offset) & (groups - 1)))
        def _(offset=offset):
            greet(rounds.at[3], along("y", offset))


    @pl.when(has_after)
    def _():
        start_layer(0)

    @pl.when(has_before)
    def _():
        start_layer(1)

    for axis, offset in near:
        greet(rounds.at[0], along(axis, offset))
    def look_up_sides(z, carry):
        look_up(z, 0)
        look_up(z, rows - 1)
        return carry

    lax.fori_loop(1, depth_size - 1, look_up_sides, 0)
    start_row(True)
    start_row(False)

    @pl.when(jnp.logical_not(has_before))
    def _():
        for y in range(rows):
            dens[0, y + 1] = zero

    @pl.when(jnp.logical_not(has_after))
    def _():
        for y in range(rows):
            dens[depth_size + 1, y + 1] = zero

    @pl.when(jnp.logical_not(has_down))
    def _():
        for z in range(depth_size):
            dens[z + 1, 0] = zero

    @pl.when(jnp.logical_not(has_up))
    def _():
        for z in range(depth_size):
            dens[z + 1, rows + 1] = zero

    def look_up_layer(z, carry):
        for y in range(1, rows - 1):
            look_up(z, y)
        return carry

    lax.fori_loop(1, depth_size - 1, look_up_layer, 0)

    rate = -2.0 / (255.0 * depth_size * groups)
    for y in range(rows):
        total = dens[1, y + 1]
        for z in range(1, depth_size):
            total = total + dens[z + 1, y + 1]
        send_pass[y] = jnp.exp(total * rate)

    def block_copy(sent, got, which, target):
        return pltpu.make_async_remote_copy(
            src_ref=sent.at[pl.ds(target * piece, piece)],
            dst_ref=got.at[me],
            send_sem=block_send.at[which],
            recv_sem=block_recv.at[which],
            device_id={"depth": target, "tile": tile},
            device_id_type=MESH,
        )

    if tuned:

        @pl.when(me < 4)
        def _():
            pl.semaphore_wait(rounds.at[3], 2)

    for offset in ring:
        block_copy(send_pass, got_pass, 0, (me + offset) & (groups - 1)).start()

    def do_colour(target):
        for r in range(piece):
            y = target * piece + r
            total = zero
            through = one
            sums = [zero, zero, zero]
            for z in range(depth_size):
                word = words[z, y]
                value = dens[z + 1, y + 1]
                total = total + value
                after = jnp.exp(total * rate)
                right = pltpu.roll(value, LANES - 1, 1)
                right = jnp.where(last_lane, pltpu.roll(right, SUBLANES - 1, 0), right)
                right = jnp.where(last_cell, 0.0, right)
                left = pltpu.roll(value, 1, 1)
                left = jnp.where(first_lane, pltpu.roll(left, 1, 0), left)
                left = jnp.where(first_cell, 0.0, left)
                dz = dens[z + 2, y + 1] - dens[z, y + 1]
                dy = dens[z + 1, y + 2] - dens[z + 1, y]
                dx = right - left
                square = dz * dz + dy * dy + dx * dx
                toward = jnp.abs(
                    dz * (0.7 * LIGHT_Z) + dy * (0.7 * LIGHT_Y) + dx * (0.7 * LIGHT_X)
                )
                shade = 0.3 + toward * lax.rsqrt(jnp.maximum(square, (0.25 * 510.0) ** 2))
                weight = (through - after) * shade
                through = after
                for c in range(3):
                    part = lax.shift_right_logical(word, 8 * (c + 1))
                    if c < 2:
                        part = part & 255
                    sums[c] = sums[c] + part.astype(jnp.float32) * weight
            row = (tile * rows + y).astype(jnp.float32)
            ramp = (0.5 + (row + 0.5) / (rows * strips)) / 255.0
            for c in range(3):
                send_colour[y, c] = sums[c] * ramp

        @pl.when(target != me)
        def _():
            block_copy(send_colour, got_colour, 1, target).start()

    def colour_pair(pair, carry):
        for kind, arrives in enumerate((has_before, has_after)):

            @pl.when(arrives)
            def _(kind=kind):
                rows_copy(2 * piece, layer_recv.at[kind, pair]).wait()

        @pl.when((pair == groups // 2 - 1) & has_down)
        def _():
            row_copy(True).wait_recv()

        @pl.when((pair == groups // 2 - 1) & has_up)
        def _():
            row_copy(False).wait_recv()

        def step(half, carry):
            do_colour(block_at(me, pair * 2 + half))
            return carry

        return lax.fori_loop(0, 2, step, carry)

    lax.fori_loop(0, groups // 2, colour_pair, 0)

    for r in range(piece):
        got_pass[me, r] = send_pass[me * piece + r]
        for c in range(3):
            got_colour[me, r, c] = send_colour[me * piece + r, c]

    if near:
        pl.semaphore_wait(rounds.at[0], len(near))
    second_round = [("z", o) for o in (2, size_z - 2) if size_z >= 8]
    for axis, offset in second_round:
        greet(rounds.at[1], along(axis, offset))
    if second_round:
        pl.semaphore_wait(rounds.at[1], len(second_round))
    third_round = [("x", o) for o in range(1, size_x) if size_z > 1]
    for axis, offset in third_round:
        greet(rounds.at[2], along(axis, offset))

    def all_but_one(ref, semaphore):
        part = ref.at[pl.ds(0, ref.shape[0] - 1)]
        return pltpu.make_async_copy(part, part, semaphore)

    def in_first(index):
        return {"depth": index >> 1, "tile": chip * 2 + (index & 1)}

    def in_second(index):
        return {"depth": me, "tile": index * 2 + core}

    stages = []
    for parts, mine, device in (
        (part_one, me * 2 + core, in_first),
        (part_two, chip, in_second),
    ):
        others = [jnp.where(k < mine, k, k + 1) for k in range(parts.shape[0] - 1)]
        stages.append((parts, mine, [device(index) for index in others]))

    all_but_one(got_pass, block_recv.at[0]).wait()
    ranks = [order[0, g] for g in range(groups)]
    through = [[got_pass[g, r] for g in range(groups)] for r in range(piece)]
    ahead = [[one] * groups for _ in range(piece)]
    for g in range(groups):
        for h in range(groups):
            if h != g:
                before = ranks[h] < ranks[g]
                for r in range(piece):
                    ahead[r][g] = ahead[r][g] * jnp.where(before, through[r][h], one)
    for r in range(piece):
        total = through[r][0]
        for g in range(1, groups):
            total = total * through[r][g]
        frame_ref[3, :, r, :] = 1.0 - total
        for g in range(groups):
            got_pass[g, r] = ahead[r][g]

    all_but_one(got_colour, block_recv.at[1]).wait()
    composite = []
    for r in range(piece):
        sums = [zero, zero, zero]
        for g in range(groups):
            factor = got_pass[g, r]
            for c in range(3):
                sums[c] = sums[c] + factor * got_colour[g, r, c]
        composite.append(sums)

    logs = zero
    for r in range(piece):
        lum = 0.2126 * composite[r][0] + 0.7152 * composite[r][1] + 0.0722 * composite[r][2]
        logs = logs + jnp.log(0.05 + lum)
    local = jnp.sum(logs, axis=0, keepdims=True)

    for stage, (parts, mine, devices) in enumerate(stages):
        parts[mine] = local
        if stage == 1 and third_round:
            pl.semaphore_wait(rounds.at[2], len(third_round))
        for device in devices:
            pltpu.make_async_remote_copy(
                src_ref=parts.at[mine],
                dst_ref=parts.at[mine],
                send_sem=sum_send.at[stage],
                recv_sem=sum_recv.at[stage],
                device_id=device,
                device_id_type=MESH,
            ).start()
        all_but_one(parts, sum_recv.at[stage]).wait()
        terms = [parts[k] for k in range(parts.shape[0])]
        while len(terms) > 1:
            terms = [a + b for a, b in zip(terms[::2], terms[1::2], strict=True)]
        local = terms[0]
    log_sum = jnp.sum(local, axis=1, keepdims=True)
    scale = jnp.exp(math.log(KEY_VALUE) - log_sum * (1.0 / (rows * strips * cols)))
    scale = jnp.broadcast_to(scale, (SUBLANES, LANES))

    for r in range(piece):
        for c in range(3):
            scaled = composite[r][c] * scale
            frame_ref[c, :, r, :] = scaled / (1.0 + scaled)

    for kind in range(4):

        @pl.when(sends[kind])
        def _(kind=kind):
            rows_copy(rows if kind < 2 else depth_size, halo_send.at[kind]).wait()

    all_but_one(got_pass, block_send.at[0]).wait()
    all_but_one(got_colour, block_send.at[1]).wait()
    all_but_one(part_one, sum_send.at[0]).wait()
    all_but_one(part_two, sum_send.at[1]).wait()


def body(labels, depth_order, opacity_table, colour_map):
    groups = lax.axis_size("depth")
    strips = lax.axis_size("tile")
    depth_size, rows, cols = labels.shape
    piece = rows // groups
    block = (SUBLANES, LANES)
    frame = pl.pallas_call(
        functools.partial(kernel, (groups, strips, depth_size, rows)),
        out_shape=pltpu.VMEM((4, SUBLANES, piece, LANES), jnp.float32),
        in_specs=[pl.BlockSpec(memory_space=pl.ANY)] * 4,
        out_specs=pl.BlockSpec(memory_space=pltpu.VMEM),
        scratch_shapes=[
            pltpu.VMEM((SUBLANES, depth_size, rows, LANES), jnp.int32),
            pltpu.SMEM((1, groups), jnp.int32),
            pltpu.VMEM((2 * LANES,), jnp.int32),
            pltpu.VMEM((3, 2 * LANES), jnp.int32),
            pltpu.VMEM((depth_size, rows) + block, jnp.int32),
            pltpu.VMEM((depth_size + 2, rows + 2) + block, jnp.float32),
            pltpu.VMEM((rows,) + block, jnp.float32),
            pltpu.VMEM((rows, 3) + block, jnp.float32),
            pltpu.VMEM((groups, piece) + block, jnp.float32),
            pltpu.VMEM((groups, piece, 3) + block, jnp.float32),
            pltpu.VMEM((groups * 2, 1, LANES), jnp.float32),
            pltpu.VMEM((strips // 2, 1, LANES), jnp.float32),
            pltpu.SemaphoreType.DMA((4,)),
            pltpu.SemaphoreType.DMA((4,)),
            pltpu.SemaphoreType.DMA((2, groups // 2)),
            pltpu.SemaphoreType.DMA((2,)),
            pltpu.SemaphoreType.DMA((2,)),
            pltpu.SemaphoreType.DMA((2,)),
            pltpu.SemaphoreType.DMA((2,)),
            pltpu.SemaphoreType.DMA((2,)),
            pltpu.SemaphoreType.REGULAR((4,)),
        ],
        compiler_params=pltpu.CompilerParams(
            collective_id=0, has_side_effects=True, vmem_limit_bytes=32 * 1024 * 1024
        ),
        name="render",
    )(*[pltpu.with_memory_space_constraint(a, pltpu.HBM) for a in (labels, depth_order, opacity_table, colour_map)])
    return jnp.swapaxes(frame, 1, 2).reshape(4, 1, piece, cols)


def solution(mesh):
    in_specs = (P("depth", "tile", None), P("tile", None), P(), P())
    out_specs = P(None, "tile", "depth", None)
    return jax.shard_map(body, mesh=mesh, in_specs=in_specs, out_specs=out_specs, check_vma=False)
```

```python
import functools
import math

import jax
import jax.numpy as jnp
from jax import lax
from jax.experimental import pallas as pl
from jax.experimental.pallas import tpu as pltpu
from jax.sharding import PartitionSpec as P

LIGHT_Z = 0.8
LIGHT_Y = 0.36
LIGHT_X = 0.48
KEY_VALUE = 0.18
SIZE_X = 4
LANES = 128
SUBLANES = 8
MESH = pl.DeviceIdType.MESH


def gathered(table, index):
    return jnp.take_along_axis(table, index, axis=1, mode="promise_in_bounds")


def image_row(labels, z, y):
    blocks, depth_size, rows, lanes = labels.shape
    flat = labels.reshape(blocks * depth_size * rows, lanes)
    return flat[pl.ds(z * rows + y, blocks, stride=depth_size * rows), :]


def kernel(
    sizes,
    labels_hbm,
    order_hbm,
    opacity_hbm,
    colour_hbm,
    frame_ref,
    labels,
    order,
    opacity,
    colour,
    words,
    dens,
    send_pass,
    send_colour,
    got_pass,
    got_colour,
    part_one,
    part_two,
    load_sem,
    halo_send,
    layer_recv,
    row_recv,
    block_send,
    block_recv,
    sum_send,
    sum_recv,
    rounds,
):
    groups, strips, depth_size, rows = sizes
    cols = SUBLANES * LANES
    piece = rows // groups
    size_x = min(SIZE_X, strips // 2)
    size_z = strips // (2 * size_x)
    me = lax.axis_index("depth")
    tile = lax.axis_index("tile")
    chip = tile >> 1
    core = tile & 1
    at_x = chip & (size_x - 1)
    at_z = lax.div(chip, size_x)
    lengths = {"y": groups, "x": size_x, "z": size_z}

    def along(axis, offset):
        if axis == "y":
            return {"depth": (me + offset) & (groups - 1), "tile": tile}
        if axis == "x":
            there = at_z * size_x + ((at_x + offset) & (size_x - 1))
        else:
            there = ((at_z + offset) & (size_z - 1)) * size_x + at_x
        return {"depth": me, "tile": there * 2 + core}

    def greet(semaphore, device):
        pl.semaphore_signal(semaphore, inc=1, device_id=device, device_id_type=MESH)

    barrier = pltpu.get_barrier_semaphore()
    has_up = tile < strips - 1
    has_down = tile > 0
    has_after = me < groups - 1
    has_before = me > 0
    ring = sorted(range(1, groups), key=lambda offset: -min(offset, groups - offset))
    near = [(a, o) for a in ("x", "z") if lengths[a] > 1 for o in sorted({1, lengths[a] - 1})]

    tuned = groups == 8

    def told_later(source, target):
        if not tuned:
            return jnp.bool_(False)
        late = ((source == 4) & (target < 3)) | ((source == 5) & (target < 4))
        return late | ((source == 7) & (target == 3))

    def tells(source, target):
        late = ((source == 4) & (target < 3)) | ((source == 5) & (target < 4))
        return late | ((source == 0) & (target == 3))

    for offset in ring:

        @pl.when(jnp.logical_not(told_later(me, (me + offset) & (groups - 1))))
        def _(offset=offset):
            greet(barrier, along("y", offset))

    @pl.when(has_up)
    def _():
        greet(barrier, {"depth": me, "tile": tile + 1})

    @pl.when(has_down)
    def _():
        greet(barrier, {"depth": me, "tile": tile - 1})

    halves = size_z == 8
    late_z = {1: at_z == 7, 7: at_z == 4} if halves else {}
    first_z = (at_z == 0) | (at_z == 3)
    early_z = {1: first_z, 7: first_z} if halves else {}

    def greet_near(semaphore, but, only=False):
        for axis, offset in near:
            special = but.get(offset) if axis == "z" else None
            if special is None:
                if not only:
                    greet(semaphore, along(axis, offset))
                continue

            @pl.when(special if only else jnp.logical_not(special))
            def _(axis=axis, offset=offset):
                greet(semaphore, along(axis, offset))

    greet_near(barrier, late_z)
    tidings = jnp.where(me < 4, 2, 0) if tuned else 0
    if halves:
        tidings = tidings + first_z.astype(jnp.int32)
    greeted = len(ring) - tidings + len(near) + has_up.astype(jnp.int32) + has_down.astype(jnp.int32)

    for block in range(SUBLANES):
        pltpu.make_async_copy(
            labels_hbm.at[:, :, pl.ds(block * LANES, LANES)], labels.at[block], load_sem.at[0]
        ).start()
    loads = [
        pltpu.make_async_copy(opacity_hbm, opacity, load_sem.at[1]),
        pltpu.make_async_copy(colour_hbm, colour, load_sem.at[2]),
        pltpu.make_async_copy(order_hbm, order, load_sem.at[3]),
    ]
    for load in loads:
        load.start()
    for load in loads:
        load.wait()

    level = [opacity[...].reshape(1, 2 * LANES)] + [colour[c : c + 1, :] for c in range(3)]
    packed = level[0] + level[1] * 256 + level[2] * 65536 + level[3] * 16777216
    low = jnp.broadcast_to(packed[:, :LANES], (SUBLANES, LANES))
    high = jnp.broadcast_to(packed[:, LANES:], (SUBLANES, LANES))
    lane = lax.broadcasted_iota(jnp.int32, (SUBLANES, LANES), 1)
    sub = lax.broadcasted_iota(jnp.int32, (SUBLANES, LANES), 0)
    first_lane, last_lane = lane == 0, lane == LANES - 1
    first_cell = first_lane & (sub == 0)
    last_cell = last_lane & (sub == SUBLANES - 1)
    zero = jnp.zeros((SUBLANES, LANES), jnp.float32)
    one = jnp.ones((SUBLANES, LANES), jnp.float32)
    pltpu.make_async_copy(labels, labels, load_sem.at[0]).wait()

    def look_up(z, y):
        label = image_row(labels, z, y)
        index = label & (LANES - 1)
        word = jnp.where(label < LANES, gathered(low, index), gathered(high, index))
        words[z, y] = word
        dens[z + 1, y + 1] = (word & 255).astype(jnp.float32)

    def block_at(depth, step):
        third = (groups - 2) // 2
        turn = lax.rem(depth + step + 1, third)
        flip = (depth + step) & 1
        return jnp.where(
            step < third,
            turn + 4,
            jnp.where(step < 5, jnp.where(flip == 0, 3, 7), jnp.where(step < 7, 2 - flip, 0)),
        )

    def start_layer(kind):
        target = me + 1 if kind == 0 else me - 1
        src, dst = (depth_size, 0) if kind == 0 else (1, depth_size + 1)
        for step in range(groups):
            part = pl.ds(block_at(target, step) * piece + 1, piece)
            pltpu.make_async_remote_copy(
                src_ref=dens.at[src, part],
                dst_ref=dens.at[dst, part],
                send_sem=halo_send.at[kind],
                recv_sem=layer_recv.at[kind, step // 2],
                device_id={"depth": target, "tile": tile},
                device_id_type=MESH,
            ).start()

    def rows_copy(count, semaphore):
        part = dens.at[0, pl.ds(0, count)]
        return pltpu.make_async_copy(part, part, semaphore)

    def row_copy(up):
        row, there = (rows, 0) if up else (1, rows + 1)
        return pltpu.make_async_remote_copy(
            src_ref=dens.at[pl.ds(1, depth_size), row],
            dst_ref=dens.at[pl.ds(1, depth_size), there],
            send_sem=halo_send.at[2 if up else 3],
            recv_sem=row_recv.at[0 if up else 1],
            device_id={"depth": me, "tile": tile + 1 if up else tile - 1},
            device_id_type=MESH,
        )

    def start_row(up):
        @pl.when(has_up if up else has_down)
        def _():
            row_copy(up).start()

    sends = (has_after, has_before, has_up, has_down)

    def look_up_ends(row, carry):
        for y in range(4):
            look_up(depth_size - 1, row * 4 + y)
            look_up(0, row * 4 + y)
        return carry

    lax.fori_loop(0, rows // 4, look_up_ends, 0)
    pl.semaphore_wait(barrier, greeted)
    for offset in ring if tuned else ():

        @pl.when(tells(me, (me + offset) & (groups - 1)))
        def _(offset=offset):
            greet(rounds.at[3], along("y", offset))


    @pl.when(has_after)
    def _():
        start_layer(0)

    @pl.when(has_before)
    def _():
        start_layer(1)

    greet_near(rounds.at[0], early_z)
    def look_up_sides(z, carry):
        look_up(z, 0)
        look_up(z, rows - 1)
        return carry

    lax.fori_loop(1, depth_size - 1, look_up_sides, 0)
    start_row(True)
    start_row(False)

    @pl.when(jnp.logical_not(has_before))
    def _():
        for y in range(rows):
            dens[0, y + 1] = zero

    @pl.when(jnp.logical_not(has_after))
    def _():
        for y in range(rows):
            dens[depth_size + 1, y + 1] = zero

    @pl.when(jnp.logical_not(has_down))
    def _():
        for z in range(depth_size):
            dens[z + 1, 0] = zero

    @pl.when(jnp.logical_not(has_up))
    def _():
        for z in range(depth_size):
            dens[z + 1, rows + 1] = zero

    def look_up_layer(z, carry):
        for y in range(1, rows - 1):
            look_up(z, y)
        return carry

    lax.fori_loop(1, depth_size - 1, look_up_layer, 0)

    rate = -2.0 / (255.0 * depth_size * groups)
    for y in range(rows):
        total = dens[1, y + 1]
        for z in range(1, depth_size):
            total = total + dens[z + 1, y + 1]
        send_pass[y] = jnp.exp(total * rate)

    def block_copy(sent, got, which, target):
        return pltpu.make_async_remote_copy(
            src_ref=sent.at[pl.ds(target * piece, piece)],
            dst_ref=got.at[me],
            send_sem=block_send.at[which],
            recv_sem=block_recv.at[which],
            device_id={"depth": target, "tile": tile},
            device_id_type=MESH,
        )

    if tuned:

        @pl.when(me < 4)
        def _():
            pl.semaphore_wait(rounds.at[3], 2)

    for offset in ring:
        block_copy(send_pass, got_pass, 0, (me + offset) & (groups - 1)).start()

    def do_colour(target):
        for r in range(piece):
            y = target * piece + r
            total = zero
            through = one
            sums = [zero, zero, zero]
            for z in range(depth_size):
                word = words[z, y]
                value = dens[z + 1, y + 1]
                total = total + value
                after = jnp.exp(total * rate)
                right = pltpu.roll(value, LANES - 1, 1)
                right = jnp.where(last_lane, pltpu.roll(right, SUBLANES - 1, 0), right)
                right = jnp.where(last_cell, 0.0, right)
                left = pltpu.roll(value, 1, 1)
                left = jnp.where(first_lane, pltpu.roll(left, 1, 0), left)
                left = jnp.where(first_cell, 0.0, left)
                dz = dens[z + 2, y + 1] - dens[z, y + 1]
                dy = dens[z + 1, y + 2] - dens[z + 1, y]
                dx = right - left
                square = dz * dz + dy * dy + dx * dx
                toward = jnp.abs(
                    dz * (0.7 * LIGHT_Z) + dy * (0.7 * LIGHT_Y) + dx * (0.7 * LIGHT_X)
                )
                shade = 0.3 + toward * lax.rsqrt(jnp.maximum(square, (0.25 * 510.0) ** 2))
                weight = (through - after) * shade
                through = after
                for c in range(3):
                    part = lax.shift_right_logical(word, 8 * (c + 1))
                    if c < 2:
                        part = part & 255
                    sums[c] = sums[c] + part.astype(jnp.float32) * weight
            row = (tile * rows + y).astype(jnp.float32)
            ramp = (0.5 + (row + 0.5) / (rows * strips)) / 255.0
            for c in range(3):
                send_colour[y, c] = sums[c] * ramp

        @pl.when(target != me)
        def _():
            block_copy(send_colour, got_colour, 1, target).start()

    def colour_pair(pair, carry):
        for kind, arrives in enumerate((has_before, has_after)):

            @pl.when(arrives)
            def _(kind=kind):
                rows_copy(2 * piece, layer_recv.at[kind, pair]).wait()

        @pl.when((pair == 1) & has_down)
        def _():
            row_copy(True).wait_recv()

        @pl.when((pair == 1) & has_up)
        def _():
            row_copy(False).wait_recv()

        def step(half, carry):
            do_colour(block_at(me, pair * 2 + half))
            return carry

        return lax.fori_loop(0, 2, step, carry)

    lax.fori_loop(0, groups // 2, colour_pair, 0)

    for r in range(piece):
        got_pass[me, r] = send_pass[me * piece + r]
        for c in range(3):
            got_colour[me, r, c] = send_colour[me * piece + r, c]

    if near:
        pl.semaphore_wait(rounds.at[0], len(near))
        greet_near(rounds.at[0], early_z, only=True)
    second_round = [("z", o) for o in (2, size_z - 2) if size_z >= 8]
    for axis, offset in second_round:
        greet(rounds.at[1], along(axis, offset))
    if second_round:
        pl.semaphore_wait(rounds.at[1], len(second_round))
    third_round = [("x", o) for o in range(1, size_x) if size_z > 1]
    for axis, offset in third_round:
        greet(rounds.at[2], along(axis, offset))

    def all_but_one(ref, semaphore):
        part = ref.at[pl.ds(0, ref.shape[0] - 1)]
        return pltpu.make_async_copy(part, part, semaphore)

    def in_first(index):
        return {"depth": index >> 1, "tile": chip * 2 + (index & 1)}

    def in_second(index):
        return {"depth": me, "tile": index * 2 + core}

    stages = []
    for parts, mine, device in (
        (part_one, me * 2 + core, in_first),
        (part_two, chip, in_second),
    ):
        others = [jnp.where(k < mine, k, k + 1) for k in range(parts.shape[0] - 1)]
        stages.append((parts, mine, [device(index) for index in others]))

    all_but_one(got_pass, block_recv.at[0]).wait()
    ranks = [order[0, g] for g in range(groups)]
    through = [[got_pass[g, r] for g in range(groups)] for r in range(piece)]
    ahead = [[one] * groups for _ in range(piece)]
    for g in range(groups):
        for h in range(groups):
            if h != g:
                before = ranks[h] < ranks[g]
                for r in range(piece):
                    ahead[r][g] = ahead[r][g] * jnp.where(before, through[r][h], one)
    for r in range(piece):
        total = through[r][0]
        for g in range(1, groups):
            total = total * through[r][g]
        frame_ref[3, :, r, :] = 1.0 - total
        for g in range(groups):
            got_pass[g, r] = ahead[r][g]

    all_but_one(got_colour, block_recv.at[1]).wait()
    composite = []
    for r in range(piece):
        sums = [zero, zero, zero]
        for g in range(groups):
            factor = got_pass[g, r]
            for c in range(3):
                sums[c] = sums[c] + factor * got_colour[g, r, c]
        composite.append(sums)

    logs = zero
    for r in range(piece):
        lum = 0.2126 * composite[r][0] + 0.7152 * composite[r][1] + 0.0722 * composite[r][2]
        logs = logs + jnp.log(0.05 + lum)
    local = jnp.sum(logs, axis=0, keepdims=True)

    for stage, (parts, mine, devices) in enumerate(stages):
        parts[mine] = local
        if stage == 1 and third_round:
            pl.semaphore_wait(rounds.at[2], len(third_round))
        for device in devices:
            pltpu.make_async_remote_copy(
                src_ref=parts.at[mine],
                dst_ref=parts.at[mine],
                send_sem=sum_send.at[stage],
                recv_sem=sum_recv.at[stage],
                device_id=device,
                device_id_type=MESH,
            ).start()
        all_but_one(parts, sum_recv.at[stage]).wait()
        terms = [parts[k] for k in range(parts.shape[0])]
        while len(terms) > 1:
            terms = [a + b for a, b in zip(terms[::2], terms[1::2], strict=True)]
        local = terms[0]
    log_sum = jnp.sum(local, axis=1, keepdims=True)
    scale = jnp.exp(math.log(KEY_VALUE) - log_sum * (1.0 / (rows * strips * cols)))
    scale = jnp.broadcast_to(scale, (SUBLANES, LANES))

    for r in range(piece):
        for c in range(3):
            scaled = composite[r][c] * scale
            frame_ref[c, :, r, :] = scaled / (1.0 + scaled)

    for kind in range(4):

        @pl.when(sends[kind])
        def _(kind=kind):
            rows_copy(rows if kind < 2 else depth_size, halo_send.at[kind]).wait()

    all_but_one(got_pass, block_send.at[0]).wait()
    all_but_one(got_colour, block_send.at[1]).wait()
    all_but_one(part_one, sum_send.at[0]).wait()
    all_but_one(part_two, sum_send.at[1]).wait()


def body(labels, depth_order, opacity_table, colour_map):
    groups = lax.axis_size("depth")
    strips = lax.axis_size("tile")
    depth_size, rows, cols = labels.shape
    piece = rows // groups
    block = (SUBLANES, LANES)
    frame = pl.pallas_call(
        functools.partial(kernel, (groups, strips, depth_size, rows)),
        out_shape=pltpu.VMEM((4, SUBLANES, piece, LANES), jnp.float32),
        in_specs=[pl.BlockSpec(memory_space=pl.ANY)] * 4,
        out_specs=pl.BlockSpec(memory_space=pltpu.VMEM),
        scratch_shapes=[
            pltpu.VMEM((SUBLANES, depth_size, rows, LANES), jnp.int32),
            pltpu.SMEM((1, groups), jnp.int32),
            pltpu.VMEM((2 * LANES,), jnp.int32),
            pltpu.VMEM((3, 2 * LANES), jnp.int32),
            pltpu.VMEM((depth_size, rows) + block, jnp.int32),
            pltpu.VMEM((depth_size + 2, rows + 2) + block, jnp.float32),
            pltpu.VMEM((rows,) + block, jnp.float32),
            pltpu.VMEM((rows, 3) + block, jnp.float32),
            pltpu.VMEM((groups, piece) + block, jnp.float32),
            pltpu.VMEM((groups, piece, 3) + block, jnp.float32),
            pltpu.VMEM((groups * 2, 1, LANES), jnp.float32),
            pltpu.VMEM((strips // 2, 1, LANES), jnp.float32),
            pltpu.SemaphoreType.DMA((4,)),
            pltpu.SemaphoreType.DMA((4,)),
            pltpu.SemaphoreType.DMA((2, groups // 2)),
            pltpu.SemaphoreType.DMA((2,)),
            pltpu.SemaphoreType.DMA((2,)),
            pltpu.SemaphoreType.DMA((2,)),
            pltpu.SemaphoreType.DMA((2,)),
            pltpu.SemaphoreType.DMA((2,)),
            pltpu.SemaphoreType.REGULAR((4,)),
        ],
        compiler_params=pltpu.CompilerParams(
            collective_id=0, has_side_effects=True, vmem_limit_bytes=32 * 1024 * 1024
        ),
        name="render",
    )(*[pltpu.with_memory_space_constraint(a, pltpu.HBM) for a in (labels, depth_order, opacity_table, colour_map)])
    return jnp.swapaxes(frame, 1, 2).reshape(4, 1, piece, cols)


def solution(mesh):
    in_specs = (P("depth", "tile", None), P("tile", None), P(), P())
    out_specs = P(None, "tile", "depth", None)
    return jax.shard_map(body, mesh=mesh, in_specs=in_specs, out_specs=out_specs, check_vma=False)
```

```python
import functools
import math

import jax
import jax.numpy as jnp
from jax import lax
from jax.experimental import pallas as pl
from jax.experimental.pallas import tpu as pltpu
from jax.sharding import PartitionSpec as P

LIGHT_Z = 0.8
LIGHT_Y = 0.36
LIGHT_X = 0.48
KEY_VALUE = 0.18
SIZE_X = 4
LANES = 128
SUBLANES = 8
MESH = pl.DeviceIdType.MESH


def gathered(table, index):
    return jnp.take_along_axis(table, index, axis=1, mode="promise_in_bounds")


def image_row(labels, z, y):
    blocks, depth_size, rows, lanes = labels.shape
    flat = labels.reshape(blocks * depth_size * rows, lanes)
    return flat[pl.ds(z * rows + y, blocks, stride=depth_size * rows), :]


def kernel(
    sizes,
    labels_hbm,
    order_hbm,
    opacity_hbm,
    colour_hbm,
    frame_ref,
    labels,
    order,
    opacity,
    colour,
    words,
    dens,
    send_pass,
    send_colour,
    got_pass,
    got_colour,
    part_one,
    part_two,
    load_sem,
    halo_send,
    layer_recv,
    row_recv,
    block_send,
    block_recv,
    sum_send,
    sum_recv,
    rounds,
):
    groups, strips, depth_size, rows = sizes
    cols = SUBLANES * LANES
    piece = rows // groups
    size_x = min(SIZE_X, strips // 2)
    size_z = strips // (2 * size_x)
    me = lax.axis_index("depth")
    tile = lax.axis_index("tile")
    chip = tile >> 1
    core = tile & 1
    at_x = chip & (size_x - 1)
    at_z = lax.div(chip, size_x)
    lengths = {"y": groups, "x": size_x, "z": size_z}

    def along(axis, offset):
        if axis == "y":
            return {"depth": (me + offset) & (groups - 1), "tile": tile}
        if axis == "x":
            there = at_z * size_x + ((at_x + offset) & (size_x - 1))
        else:
            there = ((at_z + offset) & (size_z - 1)) * size_x + at_x
        return {"depth": me, "tile": there * 2 + core}

    def greet(semaphore, device):
        pl.semaphore_signal(semaphore, inc=1, device_id=device, device_id_type=MESH)

    barrier = pltpu.get_barrier_semaphore()
    has_up = tile < strips - 1
    has_down = tile > 0
    has_after = me < groups - 1
    has_before = me > 0
    ring = sorted(range(1, groups), key=lambda offset: -min(offset, groups - offset))
    near = [(a, o) for a in ("x", "z") if lengths[a] > 1 for o in sorted({1, lengths[a] - 1})]

    tuned = groups == 8

    def told_later(source, target):
        if not tuned:
            return jnp.bool_(False)
        late = ((source == 4) & (target < 3)) | ((source == 5) & (target < 4))
        return late | ((source == 7) & (target == 3))

    def tells(source, target):
        late = ((source == 4) & (target < 3)) | ((source == 5) & (target < 4))
        return late | ((source == 0) & (target == 3))

    for offset in ring:

        @pl.when(jnp.logical_not(told_later(me, (me + offset) & (groups - 1))))
        def _(offset=offset):
            greet(barrier, along("y", offset))

    @pl.when(has_up)
    def _():
        greet(barrier, {"depth": me, "tile": tile + 1})

    @pl.when(has_down)
    def _():
        greet(barrier, {"depth": me, "tile": tile - 1})

    halves = size_z == 8
    late_z = {1: at_z == 7, 7: at_z == 4} if halves else {}
    first_z = (at_z == 0) | (at_z == 3)
    early_z = {1: first_z, 7: first_z} if halves else {}

    def greet_near(semaphore, but, only=False):
        for axis, offset in near:
            special = but.get(offset) if axis == "z" else None
            if special is None:
                if not only:
                    greet(semaphore, along(axis, offset))
                continue

            @pl.when(special if only else jnp.logical_not(special))
            def _(axis=axis, offset=offset):
                greet(semaphore, along(axis, offset))

    greet_near(barrier, late_z)
    tidings = jnp.where(me < 4, 2, 0) if tuned else 0
    if halves:
        tidings = tidings + first_z.astype(jnp.int32)
    greeted = len(ring) - tidings + len(near) + has_up.astype(jnp.int32) + has_down.astype(jnp.int32)

    for block in range(SUBLANES):
        pltpu.make_async_copy(
            labels_hbm.at[:, :, pl.ds(block * LANES, LANES)], labels.at[block], load_sem.at[0]
        ).start()
    loads = [
        pltpu.make_async_copy(opacity_hbm, opacity, load_sem.at[1]),
        pltpu.make_async_copy(colour_hbm, colour, load_sem.at[2]),
        pltpu.make_async_copy(order_hbm, order, load_sem.at[3]),
    ]
    for load in loads:
        load.start()
    for load in loads:
        load.wait()

    level = [opacity[...].reshape(1, 2 * LANES)] + [colour[c : c + 1, :] for c in range(3)]
    packed = level[0] + level[1] * 256 + level[2] * 65536 + level[3] * 16777216
    low = jnp.broadcast_to(packed[:, :LANES], (SUBLANES, LANES))
    high = jnp.broadcast_to(packed[:, LANES:], (SUBLANES, LANES))
    lane = lax.broadcasted_iota(jnp.int32, (SUBLANES, LANES), 1)
    sub = lax.broadcasted_iota(jnp.int32, (SUBLANES, LANES), 0)
    first_lane, last_lane = lane == 0, lane == LANES - 1
    first_cell = first_lane & (sub == 0)
    last_cell = last_lane & (sub == SUBLANES - 1)
    zero = jnp.zeros((SUBLANES, LANES), jnp.float32)
    one = jnp.ones((SUBLANES, LANES), jnp.float32)
    pltpu.make_async_copy(labels, labels, load_sem.at[0]).wait()

    def look_up(z, y):
        label = image_row(labels, z, y)
        index = label & (LANES - 1)
        word = jnp.where(label < LANES, gathered(low, index), gathered(high, index))
        words[z, y] = word
        dens[z + 1, y + 1] = (word & 255).astype(jnp.float32)

    def block_at(depth, step):
        third = (groups - 2) // 2
        turn = lax.rem(depth + step + 1, third)
        flip = (depth + step) & 1
        return jnp.where(
            step < third,
            turn + 4,
            jnp.where(step < 5, jnp.where(flip == 0, 3, 7), jnp.where(step < 7, 2 - flip, 0)),
        )

    def start_layer(kind):
        target = me + 1 if kind == 0 else me - 1
        src, dst = (depth_size, 0) if kind == 0 else (1, depth_size + 1)
        for step in range(groups):
            part = pl.ds(block_at(target, step) * piece + 1, piece)
            pltpu.make_async_remote_copy(
                src_ref=dens.at[src, part],
                dst_ref=dens.at[dst, part],
                send_sem=halo_send.at[kind],
                recv_sem=layer_recv.at[kind, step // 2],
                device_id={"depth": target, "tile": tile},
                device_id_type=MESH,
            ).start()

    def rows_copy(count, semaphore):
        part = dens.at[0, pl.ds(0, count)]
        return pltpu.make_async_copy(part, part, semaphore)

    def row_copy(up):
        row, there = (rows, 0) if up else (1, rows + 1)
        return pltpu.make_async_remote_copy(
            src_ref=dens.at[pl.ds(1, depth_size), row],
            dst_ref=dens.at[pl.ds(1, depth_size), there],
            send_sem=halo_send.at[2 if up else 3],
            recv_sem=row_recv.at[0 if up else 1],
            device_id={"depth": me, "tile": tile + 1 if up else tile - 1},
            device_id_type=MESH,
        )

    def start_row(up):
        @pl.when(has_up if up else has_down)
        def _():
            row_copy(up).start()

    sends = (has_after, has_before, has_up, has_down)

    def look_up_ends(row, carry):
        for y in range(4):
            look_up(depth_size - 1, row * 4 + y)
            look_up(0, row * 4 + y)
        return carry

    lax.fori_loop(0, rows // 4, look_up_ends, 0)
    pl.semaphore_wait(barrier, greeted)
    for offset in ring if tuned else ():

        @pl.when(tells(me, (me + offset) & (groups - 1)))
        def _(offset=offset):
            greet(rounds.at[3], along("y", offset))


    @pl.when(has_after)
    def _():
        start_layer(0)

    @pl.when(has_before)
    def _():
        start_layer(1)

    greet_near(rounds.at[0], early_z)
    def look_up_sides(z, carry):
        look_up(z, 0)
        look_up(z, rows - 1)
        return carry

    lax.fori_loop(1, depth_size - 1, look_up_sides, 0)
    start_row(True)
    start_row(False)

    @pl.when(jnp.logical_not(has_before))
    def _():
        for y in range(rows):
            dens[0, y + 1] = zero

    @pl.when(jnp.logical_not(has_after))
    def _():
        for y in range(rows):
            dens[depth_size + 1, y + 1] = zero

    @pl.when(jnp.logical_not(has_down))
    def _():
        for z in range(depth_size):
            dens[z + 1, 0] = zero

    @pl.when(jnp.logical_not(has_up))
    def _():
        for z in range(depth_size):
            dens[z + 1, rows + 1] = zero

    def look_up_layer(z, carry):
        for y in range(1, rows - 1):
            look_up(z, y)
        return carry

    lax.fori_loop(1, depth_size - 1, look_up_layer, 0)

    rate = -2.0 / (255.0 * depth_size * groups)
    for y in range(rows):
        total = dens[1, y + 1]
        for z in range(1, depth_size):
            total = total + dens[z + 1, y + 1]
        send_pass[y] = jnp.exp(total * rate)

    def block_copy(sent, got, which, target):
        return pltpu.make_async_remote_copy(
            src_ref=sent.at[pl.ds(target * piece, piece)],
            dst_ref=got.at[me],
            send_sem=block_send.at[which],
            recv_sem=block_recv.at[which],
            device_id={"depth": target, "tile": tile},
            device_id_type=MESH,
        )

    if tuned:

        @pl.when(me < 4)
        def _():
            pl.semaphore_wait(rounds.at[3], 2)

    for offset in ring:
        block_copy(send_pass, got_pass, 0, (me + offset) & (groups - 1)).start()

    def do_colour(target):
        for r in range(piece):
            y = target * piece + r
            total = zero
            through = one
            sums = [zero, zero, zero]
            for z in range(depth_size):
                word = words[z, y]
                value = dens[z + 1, y + 1]
                total = total + value
                after = jnp.exp(total * rate)
                right = pltpu.roll(value, LANES - 1, 1)
                right = jnp.where(last_lane, pltpu.roll(right, SUBLANES - 1, 0), right)
                right = jnp.where(last_cell, 0.0, right)
                left = pltpu.roll(value, 1, 1)
                left = jnp.where(first_lane, pltpu.roll(left, 1, 0), left)
                left = jnp.where(first_cell, 0.0, left)
                dz = dens[z + 2, y + 1] - dens[z, y + 1]
                dy = dens[z + 1, y + 2] - dens[z + 1, y]
                dx = right - left
                square = dz * dz + dy * dy + dx * dx
                toward = jnp.abs(
                    dz * (0.7 * LIGHT_Z) + dy * (0.7 * LIGHT_Y) + dx * (0.7 * LIGHT_X)
                )
                shade = 0.3 + toward * lax.rsqrt(jnp.maximum(square, (0.25 * 510.0) ** 2))
                weight = (through - after) * shade
                through = after
                for c in range(3):
                    part = lax.shift_right_logical(word, 8 * (c + 1))
                    if c < 2:
                        part = part & 255
                    sums[c] = sums[c] + part.astype(jnp.float32) * weight
            row = (tile * rows + y).astype(jnp.float32)
            ramp = (0.5 + (row + 0.5) / (rows * strips)) / 255.0
            for c in range(3):
                send_colour[y, c] = sums[c] * ramp

        @pl.when(target != me)
        def _():
            block_copy(send_colour, got_colour, 1, target).start()

    def colour_pair(pair, carry):
        for kind, arrives in enumerate((has_before, has_after)):

            @pl.when(arrives)
            def _(kind=kind):
                rows_copy(2 * piece, layer_recv.at[kind, pair]).wait()

        @pl.when((pair == 1) & has_down)
        def _():
            row_copy(True).wait_recv()

        @pl.when((pair == 1) & has_up)
        def _():
            row_copy(False).wait_recv()

        def step(half, carry):
            do_colour(block_at(me, pair * 2 + half))
            return carry

        return lax.fori_loop(0, 2, step, carry)

    lax.fori_loop(0, groups // 2, colour_pair, 0)

    for r in range(piece):
        got_pass[me, r] = send_pass[me * piece + r]
        for c in range(3):
            got_colour[me, r, c] = send_colour[me * piece + r, c]

    if near:
        pl.semaphore_wait(rounds.at[0], len(near))
        greet_near(rounds.at[0], early_z, only=True)
    second_round = [("z", o) for o in (2, size_z - 2) if size_z >= 8]
    for axis, offset in second_round:
        greet(rounds.at[1], along(axis, offset))
    if second_round:
        pl.semaphore_wait(rounds.at[1], len(second_round))
    third_round = [("x", o) for o in range(1, size_x) if size_z > 1]
    for axis, offset in third_round:
        greet(rounds.at[2], along(axis, offset))

    def all_but_one(ref, semaphore):
        part = ref.at[pl.ds(0, ref.shape[0] - 1)]
        return pltpu.make_async_copy(part, part, semaphore)

    def in_first(index):
        return {"depth": index >> 1, "tile": chip * 2 + (index & 1)}

    def in_second(index):
        return {"depth": me, "tile": index * 2 + core}

    stages = []
    for parts, mine, device in (
        (part_one, me * 2 + core, in_first),
        (part_two, chip, in_second),
    ):
        others = [jnp.where(k < mine, k, k + 1) for k in range(parts.shape[0] - 1)]
        stages.append((parts, mine, [device(index) for index in others]))

    all_but_one(got_pass, block_recv.at[0]).wait()
    ranks = [order[0, g] for g in range(groups)]
    through = [[got_pass[g, r] for g in range(groups)] for r in range(piece)]
    ahead = [[one] * groups for _ in range(piece)]
    for g in range(groups):
        for h in range(groups):
            if h != g:
                before = ranks[h] < ranks[g]
                for r in range(piece):
                    ahead[r][g] = ahead[r][g] * jnp.where(before, through[r][h], one)
    for r in range(piece):
        total = through[r][0]
        for g in range(1, groups):
            total = total * through[r][g]
        frame_ref[3, :, r, :] = 1.0 - total
        for g in range(groups):
            got_pass[g, r] = ahead[r][g]

    all_but_one(got_colour, block_recv.at[1]).wait()
    composite = []
    for r in range(piece):
        sums = [zero, zero, zero]
        for g in range(groups):
            factor = got_pass[g, r]
            for c in range(3):
                sums[c] = sums[c] + factor * got_colour[g, r, c]
        composite.append(sums)

    logs = zero
    for r in range(piece):
        lum = 0.2126 * composite[r][0] + 0.7152 * composite[r][1] + 0.0722 * composite[r][2]
        logs = logs + jnp.log(0.05 + lum)
    local = jnp.sum(logs, axis=0, keepdims=True)

    for stage, (parts, mine, devices) in enumerate(stages):
        parts[mine] = local
        if stage == 1 and third_round:
            pl.semaphore_wait(rounds.at[2], len(third_round))
        for device in devices:
            pltpu.make_async_remote_copy(
                src_ref=parts.at[mine],
                dst_ref=parts.at[mine],
                send_sem=sum_send.at[stage],
                recv_sem=sum_recv.at[stage],
                device_id=device,
                device_id_type=MESH,
            ).start()
        if stage == 1:
            for kind in range(4):

                @pl.when(sends[kind])
                def _(kind=kind):
                    rows_copy(rows if kind < 2 else depth_size, halo_send.at[kind]).wait()

            all_but_one(got_pass, block_send.at[0]).wait()
            all_but_one(got_colour, block_send.at[1]).wait()
        all_but_one(parts, sum_send.at[stage]).wait()
        all_but_one(parts, sum_recv.at[stage]).wait()
        terms = [parts[k] for k in range(parts.shape[0])]
        while len(terms) > 1:
            terms = [a + b for a, b in zip(terms[::2], terms[1::2], strict=True)]
        local = terms[0]
    log_sum = jnp.sum(local, axis=1, keepdims=True)
    scale = jnp.exp(math.log(KEY_VALUE) - log_sum * (1.0 / (rows * strips * cols)))
    scale = jnp.broadcast_to(scale, (SUBLANES, LANES))

    for r in range(piece):
        for c in range(3):
            scaled = composite[r][c] * scale
            frame_ref[c, :, r, :] = scaled / (1.0 + scaled)


def body(labels, depth_order, opacity_table, colour_map):
    groups = lax.axis_size("depth")
    strips = lax.axis_size("tile")
    depth_size, rows, cols = labels.shape
    piece = rows // groups
    block = (SUBLANES, LANES)
    frame = pl.pallas_call(
        functools.partial(kernel, (groups, strips, depth_size, rows)),
        out_shape=pltpu.VMEM((4, SUBLANES, piece, LANES), jnp.float32),
        in_specs=[pl.BlockSpec(memory_space=pl.ANY)] * 4,
        out_specs=pl.BlockSpec(memory_space=pltpu.VMEM),
        scratch_shapes=[
            pltpu.VMEM((SUBLANES, depth_size, rows, LANES), jnp.int32),
            pltpu.SMEM((1, groups), jnp.int32),
            pltpu.VMEM((2 * LANES,), jnp.int32),
            pltpu.VMEM((3, 2 * LANES), jnp.int32),
            pltpu.VMEM((depth_size, rows) + block, jnp.int32),
            pltpu.VMEM((depth_size + 2, rows + 2) + block, jnp.float32),
            pltpu.VMEM((rows,) + block, jnp.float32),
            pltpu.VMEM((rows, 3) + block, jnp.float32),
            pltpu.VMEM((groups, piece) + block, jnp.float32),
            pltpu.VMEM((groups, piece, 3) + block, jnp.float32),
            pltpu.VMEM((groups * 2, 1, LANES), jnp.float32),
            pltpu.VMEM((strips // 2, 1, LANES), jnp.float32),
            pltpu.SemaphoreType.DMA((4,)),
            pltpu.SemaphoreType.DMA((4,)),
            pltpu.SemaphoreType.DMA((2, groups // 2)),
            pltpu.SemaphoreType.DMA((2,)),
            pltpu.SemaphoreType.DMA((2,)),
            pltpu.SemaphoreType.DMA((2,)),
            pltpu.SemaphoreType.DMA((2,)),
            pltpu.SemaphoreType.DMA((2,)),
            pltpu.SemaphoreType.REGULAR((4,)),
        ],
        compiler_params=pltpu.CompilerParams(
            collective_id=0, has_side_effects=True, vmem_limit_bytes=32 * 1024 * 1024
        ),
        name="render",
    )(*[pltpu.with_memory_space_constraint(a, pltpu.HBM) for a in (labels, depth_order, opacity_table, colour_map)])
    return jnp.swapaxes(frame, 1, 2).reshape(4, 1, piece, cols)


def solution(mesh):
    in_specs = (P("depth", "tile", None), P("tile", None), P(), P())
    out_specs = P(None, "tile", "depth", None)
    return jax.shard_map(body, mesh=mesh, in_specs=in_specs, out_specs=out_specs, check_vma=False)
```
